256 devices in a mesh: group: 8 (over x, core), rows: 32 (over y, z).
Axes of the slice: x: 4, y: 4, z: 8, core: 2. Of those that a mesh axis runs over, the one named last changes fastest.
Arguments:
- embeddings: float32 [131072, 4096], P(('group', 'rows')), may hold values from -600 to 600, as said below
- sketch_matrix: float32 [4096, 256], replicated, may hold values from -0.09375 to 0.09375
Outputs:
- left_basis: float32 [131072, 256], P(('group', 'rows'))
- right_basis: float32 [4096, 256], P('rows')
The draws below stay inside these ranges and needn't reach their ends.
Inputs may be any that keep to these rules, and one draw needn't show every extreme that they name: `embeddings`: Real-valued entries.
All inputs are finite; a program needn't handle non-finite values.
Results may differ from the reference program's by a relative error of at most 0.00023.
Values sent between devices are 32-bit elements; how exact they have to be, the bound alone decides.
No kernel may reach another device: no remote copies, remote signals or barrier semaphores. Data moves between devices by JAX's collectives and lax.ppermute only.
A program may use at most 64 MiB of HBM per device.

```python
import math
import jax
import jax.numpy as jnp
from jax import lax

EMBED = 4096
RANK = 256
PSTEPS = 6
GROUP_ROWS = 16384
TOTAL_ROWS = 131072


def draw_embeddings(key, part):
    key = jax.random.fold_in(key, 11)
    noise_key, row_key, col_key = jax.random.split(key, 3)
    row_index = jnp.arange(TOTAL_ROWS)
    in_group = (row_index % GROUP_ROWS).astype(jnp.float32) / GROUP_ROWS
    row_ramp = (1.0 + 2.0 * in_group) * (1.0 + 2.0 * row_index.astype(jnp.float32) / TOTAL_ROWS)
    col_scale = jnp.exp(jax.random.uniform(col_key, (EMBED,), jnp.float32, math.log(0.5), math.log(5.0)))
    noise_part = jnp.clip(jax.random.normal(noise_key, (TOTAL_ROWS, EMBED), jnp.float32), -5.0, 5.0)
    rough_scale = jnp.exp(jax.random.uniform(row_key, (TOTAL_ROWS,), jnp.float32, 0.0, math.log(2.5)))
    return (noise_part * (row_ramp * rough_scale)[:, None] * col_scale[None, :]).astype(jnp.float32)


def gaussian(rng, dims, deviation, bound, kind=jnp.bfloat16):
    return jnp.clip(deviation * jax.random.normal(rng, dims, jnp.float32), -bound, bound).astype(kind)


def setup_inputs(seed: int = 0) -> dict:
    keys = jax.random.split(jax.random.key(seed), 3)
    embeddings = draw_embeddings(jax.random.fold_in(keys[2], 71), 0)
    sketch_matrix = gaussian(keys[1], (EMBED, RANK), EMBED ** -0.5, 0.09375, jnp.float32)
    return {"embeddings": embeddings, "sketch_matrix": sketch_matrix}


HIGHEST_PRECISION = lax.Precision.HIGHEST

def matmul(left_side, right_side):
    return jnp.dot(left_side.astype(jnp.float32), right_side.astype(jnp.float32), precision=HIGHEST_PRECISION, preferred_element_type=jnp.float32)

def inner_rows(left_side, right_side):
    return lax.dot_general(left_side.astype(jnp.float32), right_side.astype(jnp.float32), (((0,), (0,)), ((), ())), precision=HIGHEST_PRECISION, preferred_element_type=jnp.float32)

def reference(embeddings, sketch_matrix):
    sketch = matmul(embeddings, sketch_matrix)
    lower = jnp.linalg.cholesky(inner_rows(sketch, sketch))
    identity = jnp.eye(RANK, dtype=jnp.float32)
    inverse_upper = jax.scipy.linalg.solve_triangular(lower, identity, lower=True).T
    basis = matmul(sketch, inverse_upper)
    projected = inner_rows(embeddings, basis)
    cross = inner_rows(projected, projected)
    frob = jnp.sqrt(jnp.sum(cross * cross))
    current = cross / frob
    whitening = identity
    for turn_index in range(PSTEPS):
        middle = 1.5 * identity - 0.5 * matmul(whitening, current)
        current = matmul(current, middle)
        whitening = matmul(middle, whitening)
    right_basis = matmul(projected, whitening.T) * jnp.sqrt(EMBED / frob)
    left_basis = basis * math.sqrt(TOTAL_ROWS)
    return (left_basis, right_basis)
```

```python
import math

import jax
import jax.numpy as jnp
from jax import lax
from jax.sharding import PartitionSpec as P

PSTEPS = 6
BOTH = ("group", "rows")
NX, NC, NY, NZ = 4, 2, 4, 8

HIGH = lax.Precision.HIGH
HIGHEST = lax.Precision.HIGHEST


def dot(a, b, dims, precision):
    return lax.dot_general(
        a, b, (dims, ((), ())), precision=precision, preferred_element_type=jnp.float32
    )


def nn(a, b, precision=HIGHEST):
    return dot(a, b, ((1,), (0,)), precision)


def tn(a, b, precision=HIGHEST):
    return dot(a, b, ((0,), (0,)), precision)


def nt(a, b, precision=HIGHEST):
    return dot(a, b, ((1,), (1,)), precision)


def route(move):
    pairs = []
    for x in range(NX):
        for c in range(NC):
            for y in range(NY):
                for z in range(NZ):
                    tx, tc, ty, tz = move(x, c, y, z)
                    source = (x * NC + c) * NY * NZ + y * NZ + z
                    pairs.append((source, (tx * NC + tc) * NY * NZ + ty * NZ + tz))
    return pairs


def to_core(block):
    return lax.ppermute(block, BOTH, route(lambda x, c, y, z: (x, 1 - c, y, z)))


def along_x(block, flip):
    return lax.ppermute(block, BOTH, route(lambda x, c, y, z: (x ^ flip, c, y, z)))


def along_first(block, flip):
    def move(x, c, y, z):
        return (x, c, y ^ flip, z) if c == 0 else (x ^ flip, c, y, z)

    return lax.ppermute(block, BOTH, route(move))


def along_second(block, flip):
    def move(x, c, y, z):
        return (x ^ flip, c, y, z) if c == 0 else (x, c, y ^ flip, z)

    return lax.ppermute(block, BOTH, route(move))


def pick(blocks, index):
    return lax.dynamic_index_in_dim(blocks, index, 0, keepdims=False)


def ring_scatter(blocks, here, send):
    half = blocks.shape[-1] // 2
    rel = [pick(blocks, here ^ r) for r in range(4)]
    a = [block[..., :half] for block in rel]
    b = [block[..., half:] for block in rel]
    got_a = send(jnp.stack([a[1], a[2]]), 1)
    got_b = send(jnp.stack([b[3], b[2]]), 3)
    pass_a = send(a[3] + got_a[1], 3)
    pass_b = send(b[1] + got_b[1], 1)
    return jnp.concatenate([a[0] + got_a[0] + pass_a, b[0] + got_b[0] + pass_b], axis=-1)


def per_device(embeddings, sketch_matrix):
    rank = sketch_matrix.shape[1]
    width = embeddings.shape[1]
    total_rows = embeddings.shape[0] * lax.axis_size("group") * lax.axis_size("rows")
    group = lax.axis_index("group")
    rows = lax.axis_index("rows")
    x, c = group // NC, group % NC
    y, z = rows // NZ, rows % NZ
    share = width // (NX * NC * NY * NZ)

    sketch = nn(embeddings, sketch_matrix, HIGH)
    gram = tn(sketch, sketch)
    product = tn(embeddings, sketch, HIGH)

    parts = product.reshape(NY, NZ, NX, NC, share, rank)
    grams = gram.reshape(NX, NC, NY, NZ, rank)

    def half_of(core):
        if core == 0:
            m = parts[:, :, :, 0].transpose(0, 2, 1, 3, 4)
            g = grams[:, 0].transpose(1, 0, 2, 3)
        else:
            m = parts[:, :, :, 1].transpose(2, 0, 1, 3, 4)
            g = grams[:, 1]
        return jnp.concatenate([m.reshape(4, 4, NZ * share, rank), g], axis=2)

    half_0, half_1 = half_of(0), half_of(1)
    first_core = c == 0
    keep = jnp.where(first_core, half_0, half_1)
    other = jnp.where(first_core, half_1, half_0)
    chip = keep + to_core(other)
    first = jnp.where(first_core, y, x)
    second = jnp.where(first_core, x, y)
    line = ring_scatter(chip, first, along_first)
    column = ring_scatter(line, second, along_second)
    blocks = jnp.concatenate(
        [column[: NZ * share].reshape(NZ, share, rank), column[NZ * share :][:, None]], axis=1
    )
    z_groups = [[i * NZ + j for j in range(NZ)] for i in range(NY)]
    blocks = lax.all_to_all(blocks, "rows", 0, 0, tiled=True, axis_index_groups=z_groups)
    own = jnp.sum(blocks, axis=0)
    own_product, own_gram = own[:share], own[share:]

    from_core = to_core(own_product)
    pair = jnp.concatenate(
        [
            jnp.where(first_core, own_product, from_core),
            jnp.where(first_core, from_core, own_product),
        ]
    )
    around = jnp.stack([pair] + [along_x(pair, r) for r in (1, 2, 3)])
    block_rows = jnp.concatenate([pick(around, x ^ r) for r in range(4)])

    inner = tn(own_product, own_product)
    packet = jnp.concatenate([inner, jnp.broadcast_to(own_gram, inner.shape)], axis=1)
    packet = lax.all_to_all(packet, BOTH, 0, 0, tiled=True)
    gram = packet[:, rank:]
    inner_row = jnp.sum(packet[:, :rank], axis=0, keepdims=True)
    inner = lax.all_to_all(jnp.broadcast_to(inner_row, inner.shape), BOTH, 0, 0, tiled=True)

    identity = jnp.eye(rank, dtype=jnp.float32)
    lower = jnp.linalg.cholesky(gram, symmetrize_input=False)
    inverse = jax.scipy.linalg.solve_triangular(lower, identity, lower=True)

    left_basis = nt(sketch, inverse * math.sqrt(total_rows))
    projected = nt(block_rows, inverse)
    cross = nt(nn(inverse, inner), inverse)
    frob = jnp.sqrt(jnp.sum(cross * cross))
    now = cross / frob
    for step in range(PSTEPS):
        middle = 1.5 * identity - 0.5 * now
        projected = nt(projected, middle)
        if step < PSTEPS - 1:
            now = nn(nn(middle, now), middle)
    right_basis = projected * jnp.sqrt(width / frob)
    return (left_basis, right_basis)


def solution(mesh):
    placed = (P(BOTH, None), P())
    return jax.shard_map(
        per_device,
        mesh=mesh,
        in_specs=placed,
        out_specs=(P(BOTH, None), P("rows", None)),
        check_vma=False,
    )
```

```python
import functools
import math

import jax
import jax.numpy as jnp
from jax import lax
from jax.experimental import pallas as pl
from jax.experimental.pallas import tpu as pltpu
from jax.sharding import Mesh
from jax.sharding import PartitionSpec as P

PSTEPS = 6
NX, NC, NY, NZ = 4, 2, 4, 8
AXES = ("x", "c", "y", "z")
CHIPS = ("x", "y", "z")
PANEL, GROUP, LANES = 32, 8, 128
HIGHEST = lax.Precision.HIGHEST
VMEM_LIMIT = 48 * 2**20


def dot(a, b, dims, precision=None):
    return lax.dot_general(
        a, b, (dims, ((), ())), precision=precision, preferred_element_type=jnp.float32
    )


def nn(a, b):
    return dot(a, b, ((1,), (0,)), HIGHEST)


def tn(a, b):
    return dot(a, b, ((0,), (0,)), HIGHEST)


def nt(a, b):
    return dot(a, b, ((1,), (1,)), HIGHEST)


def split(value):
    high = value.astype(jnp.bfloat16)
    return high, (value - high.astype(jnp.float32)).astype(jnp.bfloat16)


def three(a, b, dims):
    return dot(a[0], b[0], dims) + (dot(a[0], b[1], dims) + dot(a[1], b[0], dims))


def products_kernel(
    core_ref, emb_ref, matrix_ref, sketch_ref, keep_ref, send_ref, high, low, gram, s_high, s_low
):
    step = pl.program_id(0)
    rank = matrix_ref.shape[1]

    @pl.when(step < NY)
    def _():
        parts = split(emb_ref[...])
        high[step], low[step] = parts
        term = three(parts, split(matrix_ref[...]), ((1,), (0,)))

        @pl.when(step == 0)
        def _():
            sketch_ref[...] = term

        @pl.when(step > 0)
        def _():
            sketch_ref[...] += term

    @pl.when(step == NY)
    def _():
        sketch = sketch_ref[...]
        s_high[...], s_low[...] = split(sketch)
        gram[...] = tn(sketch, sketch)

    @pl.when(step >= NY)
    def _():
        y = step - NY
        product = three((high[y], low[y]), (s_high[...], s_low[...]), ((0,), (0,)))
        product = product.reshape(NZ, NX, NC, -1, rank)
        first = core_ref[0] == 0
        for x in range(NX):
            halves = [product[:, x, c].reshape(-1, rank) for c in range(NC)]
            extra = [
                gram[pl.ds(pl.multiple_of(NZ * ((c * NX + x) * NY + y), NZ), NZ), :]
                for c in range(NC)
            ]
            size = halves[0].shape[0]
            keep_ref[0, x, :size, :] = jnp.where(first, halves[0], halves[1])
            send_ref[0, x, :size, :] = jnp.where(first, halves[1], halves[0])
            keep_ref[0, x, size:, :] = jnp.where(first, extra[0], extra[1])
            send_ref[0, x, size:, :] = jnp.where(first, extra[1], extra[0])


def products(core, embeddings, matrix):
    rows, width = embeddings.shape
    rank = matrix.shape[1]
    wide = width // NY
    piece = wide // (NX * NC) + NZ
    blocks = jax.ShapeDtypeStruct((NY, NX, piece, rank), jnp.float32)
    spec = pl.BlockSpec((1, NX, piece, rank), lambda i: (jnp.maximum(i - NY, 0), 0, 0, 0))
    return pl.pallas_call(
        products_kernel,
        grid=(2 * NY,),
        out_shape=(jax.ShapeDtypeStruct((rows, rank), jnp.float32), blocks, blocks),
        in_specs=[
            pl.BlockSpec(memory_space=pltpu.SMEM),
            pl.BlockSpec((rows, wide), lambda i: (0, jnp.minimum(i, NY - 1))),
            pl.BlockSpec((wide, rank), lambda i: (jnp.minimum(i, NY - 1), 0)),
        ],
        out_specs=(pl.BlockSpec((rows, rank), lambda i: (0, 0)), spec, spec),
        scratch_shapes=[
            pltpu.VMEM((NY, rows, wide), jnp.bfloat16),
            pltpu.VMEM((NY, rows, wide), jnp.bfloat16),
            pltpu.VMEM((rank, rank), jnp.float32),
            pltpu.VMEM((rows, rank), jnp.bfloat16),
            pltpu.VMEM((rows, rank), jnp.bfloat16),
        ],
        compiler_params=pltpu.CompilerParams(vmem_limit_bytes=VMEM_LIMIT),
        cost_estimate=pl.CostEstimate(
            flops=12 * rows * width * rank, bytes_accessed=24 * 2**20, transcendentals=0
        ),
    )(core, embeddings, matrix)


def join(core_ref, mine_ref, other_ref, out_ref):
    half = mine_ref.shape[0]
    first = core_ref[0] == 0
    out_ref[:half, :] = jnp.where(first, mine_ref[...], other_ref[...])
    out_ref[half:, :] = jnp.where(first, other_ref[...], mine_ref[...])


def eliminate(out_ref, left, right):
    order = left.shape[0]
    sub = lax.broadcasted_iota(jnp.int32, (GROUP, LANES), 0)
    halves = order // LANES
    for start in range(0, order, PANEL):
        home = start // LANES
        rows = pl.ds(start, PANEL)
        left_at = list(range(home, halves))
        right_at = list(range(0, home + 1))
        tiles = [left[rows, pl.ds(h * LANES, LANES)] for h in left_at]
        tiles += [right[rows, pl.ds(h * LANES, LANES)] for h in right_at]
        done = [[] for _ in tiles]
        pivots = []
        for group in range(0, PANEL, GROUP):
            lane = start + group - home * LANES
            tall = tiles[0].shape[0]
            cols = [
                jnp.broadcast_to(tiles[0][:, lane + m : lane + m + 1], (tall, LANES))
                for m in range(GROUP)
            ]
            for j in range(GROUP):
                pivot = cols[j][j : j + 1, :]
                pivots.append(pivot)
                factor = cols[j] * (1.0 / pivot)
                top = jnp.where(sub > j, factor[:GROUP], 0.0)
                factor = top if tall == GROUP else jnp.concatenate([top, factor[GROUP:]], axis=0)
                tiles = [t - factor * t[j : j + 1, :] for t in tiles]
                cols = [
                    q if m <= j else q - factor * q[j : j + 1, :] for m, q in enumerate(cols)
                ]
            for i, t in enumerate(tiles):
                done[i].append(t[:GROUP])
            tiles = [t[GROUP:] for t in tiles]
        scale = lax.rsqrt(jnp.concatenate(pivots, axis=0))
        full = [jnp.concatenate(d, axis=0) * scale for d in done]
        for h, t in zip(right_at, full[len(left_at) :]):
            out_ref[rows, pl.ds(h * LANES, LANES)] = t
        below = start + PANEL
        for i, h in enumerate(left_at):
            first = max(below, h * LANES)
            if first >= (h + 1) * LANES:
                continue
            target = pl.ds(first, (h + 1) * LANES - first)
            flipped = full[i].T[first - h * LANES :]
            for k, g in enumerate(left_at):
                if g >= h:
                    left[target, pl.ds(g * LANES, LANES)] -= nn(flipped, full[k])
            for k, g in enumerate(right_at):
                right[target, pl.ds(g * LANES, LANES)] -= nn(flipped, full[len(left_at) + k])


def basis_kernel(
    scale, core_ref, mine_ref, other_ref, sketch_ref, rows_ref, inverse_ref, basis_ref, out_ref,
    left, right,
):
    order = left.shape[0]
    join(core_ref, mine_ref, other_ref, left)
    across = lax.broadcasted_iota(jnp.int32, (order, order), 1)
    down = lax.broadcasted_iota(jnp.int32, (order, order), 0)
    right[...] = jnp.where(across == down, 1.0, 0.0)
    inverse_ref[...] = jnp.zeros_like(inverse_ref)
    eliminate(inverse_ref, left, right)
    inverse = inverse_ref[...]
    basis_ref[...] = nt(sketch_ref[...], inverse) * scale
    out_ref[...] = nt(rows_ref[...], inverse)


def basis(core, mine, other, sketch, block_rows, scale):
    order = sketch.shape[1]
    return pl.pallas_call(
        functools.partial(basis_kernel, scale),
        out_shape=(
            jax.ShapeDtypeStruct((order, order), jnp.float32),
            jax.ShapeDtypeStruct(sketch.shape, jnp.float32),
            jax.ShapeDtypeStruct(block_rows.shape, jnp.float32),
        ),
        in_specs=[pl.BlockSpec(memory_space=pltpu.SMEM)]
        + [pl.BlockSpec(memory_space=pltpu.VMEM)] * 4,
        scratch_shapes=[pltpu.VMEM((order, order), jnp.float32)] * 2,
        cost_estimate=pl.CostEstimate(flops=10**10, bytes_accessed=2**21, transcendentals=0),
    )(core, mine, other, sketch, block_rows)


def whiten_kernel(width, core_ref, mine_ref, other_ref, inverse_ref, rows_ref, out_ref, inner):
    join(core_ref, mine_ref, other_ref, inner)
    inverse = inverse_ref[...]
    order = inverse.shape[0]
    across = lax.broadcasted_iota(jnp.int32, (order, order), 1)
    down = lax.broadcasted_iota(jnp.int32, (order, order), 0)
    diagonal = jnp.where(across == down, 1.5, 0.0)
    cross = nt(nn(inverse, inner[...]), inverse)
    squares = jnp.sum(cross * cross, axis=0, keepdims=True)
    frob = jnp.sqrt(jnp.sum(squares, axis=1, keepdims=True))
    now = cross / frob
    projected = rows_ref[...] * jnp.sqrt(width / frob)
    for step in range(PSTEPS):
        middle = diagonal - 0.5 * now
        projected = nn(projected, middle)
        if step < PSTEPS - 1:
            now = nn(nn(middle, now), middle)
    out_ref[...] = projected


def whiten(core, mine, other, inverse, block_rows, width):
    order = inverse.shape[0]
    return pl.pallas_call(
        functools.partial(whiten_kernel, width),
        out_shape=jax.ShapeDtypeStruct(block_rows.shape, jnp.float32),
        in_specs=[pl.BlockSpec(memory_space=pltpu.SMEM)]
        + [pl.BlockSpec(memory_space=pltpu.VMEM)] * 4,
        scratch_shapes=[pltpu.VMEM((order, order), jnp.float32)],
        cost_estimate=pl.CostEstimate(flops=10**10, bytes_accessed=2**20, transcendentals=0),
    )(core, mine, other, inverse, block_rows)


def to_core(block):
    return lax.ppermute(block, "c", [(0, 1), (1, 0)])


def along_x(block, flip):
    return lax.ppermute(block, "x", [(x, x ^ flip) for x in range(NX)])


def exchange(blocks, axes):
    return lax.all_to_all(blocks, axes, 0, 0, tiled=True)


def per_device(embeddings, sketch_matrix):
    rank = sketch_matrix.shape[1]
    width = embeddings.shape[1]
    share = width // (NX * NC * NY * NZ)
    total_rows = embeddings.shape[0] * NX * NC * NY * NZ
    chips = NX * NY * NZ
    x, c = lax.axis_index("x"), lax.axis_index("c")
    first_core = c == 0
    core = c.reshape(1).astype(jnp.int32)

    sketch, keep, send = products(core, embeddings, sketch_matrix)
    chip = (keep + to_core(send)).reshape(NY * NX, -1, rank)
    line = jnp.sum(exchange(chip, ("y", "x")), axis=0)
    size = NZ * share
    line = jnp.concatenate([line[:size].reshape(NZ, share, rank), line[size:][:, None]], axis=1)
    own = jnp.sum(exchange(line, "z"), axis=0)
    own_product, own_gram = own[:share], own[share:]

    from_core = to_core(own_product)
    pair = jnp.concatenate(
        [
            jnp.where(first_core, own_product, from_core),
            jnp.where(first_core, from_core, own_product),
        ]
    )
    around = jnp.stack([pair] + [along_x(pair, r) for r in (1, 2, 3)])
    block_rows = jnp.concatenate(
        [lax.dynamic_index_in_dim(around, x ^ r, 0, keepdims=False) for r in range(NX)]
    )

    half = jnp.where(first_core, pair[:, :chips], pair[:, chips:])
    inner = tn(half, pair)
    packet = jnp.concatenate([inner, jnp.broadcast_to(own_gram, inner.shape)], axis=1)
    packet = exchange(packet, CHIPS)
    gram = packet[:, rank:]
    inner_row = jnp.sum(packet[:, :rank], axis=0, keepdims=True)
    inner = exchange(jnp.broadcast_to(inner_row, inner.shape), CHIPS)

    inverse, left_basis, projected = basis(
        core, gram, to_core(gram), sketch, block_rows, math.sqrt(total_rows)
    )
    right_basis = whiten(core, inner, to_core(inner), inverse, projected, width)
    return (left_basis, right_basis)


def solution(mesh):
    fine = Mesh(mesh.devices.reshape(NX, NC, NY, NZ), AXES)
    return jax.shard_map(
        per_device,
        mesh=fine,
        in_specs=(P(AXES, None), P()),
        out_specs=(P(AXES, None), P(("y", "z"), None)),
        check_vma=False,
    )
```

```python
import functools
import math

import jax
import jax.numpy as jnp
from jax import lax
from jax.experimental import pallas as pl
from jax.experimental.pallas import tpu as pltpu
from jax.sharding import Mesh
from jax.sharding import PartitionSpec as P

PSTEPS = 6
NX, NC, NY, NZ = 4, 2, 4, 8
AXES = ("x", "c", "y", "z")
CHIPS = ("x", "y", "z")
PANEL, GROUP, LANES = 32, 8, 128
HIGHEST = lax.Precision.HIGHEST
VMEM_LIMIT = 48 * 2**20
NN, TN, NT = ((1,), (0,)), ((0,), (0,)), ((1,), (1,))


def dot(a, b, dims, precision=None):
    return lax.dot_general(
        a, b, (dims, ((), ())), precision=precision, preferred_element_type=jnp.float32
    )


def nn(a, b):
    return dot(a, b, ((1,), (0,)), HIGHEST)


def tn(a, b):
    return dot(a, b, ((0,), (0,)), HIGHEST)


def nt(a, b):
    return dot(a, b, ((1,), (1,)), HIGHEST)


def split(value):
    high = value.astype(jnp.bfloat16)
    return high, (value - high.astype(jnp.float32)).astype(jnp.bfloat16)


def three(a, b, dims):
    return dot(a[0], b[0], dims) + (dot(a[0], b[1], dims) + dot(a[1], b[0], dims))


def products_kernel(
    core_ref, emb_ref, matrix_ref, sketch_ref, keep_ref, send_ref, high, low, gram, s_high, s_low
):
    step = pl.program_id(0)
    rank = matrix_ref.shape[1]

    @pl.when(step < NY)
    def _():
        parts = split(emb_ref[...])
        high[step], low[step] = parts
        term = three(parts, split(matrix_ref[...]), ((1,), (0,)))

        @pl.when(step == 0)
        def _():
            sketch_ref[...] = term

        @pl.when(step > 0)
        def _():
            sketch_ref[...] += term

    @pl.when(step == NY)
    def _():
        sketch = sketch_ref[...]
        s_high[...], s_low[...] = split(sketch)
        gram[...] = tn(sketch, sketch)

    @pl.when(step >= NY)
    def _():
        y = step - NY
        product = three((high[y], low[y]), (s_high[...], s_low[...]), ((0,), (0,)))
        product = product.reshape(NZ, NX, NC, -1, rank)
        first = core_ref[0] == 0
        for x in range(NX):
            halves = [product[:, x, c].reshape(-1, rank) for c in range(NC)]
            extra = [
                gram[pl.ds(pl.multiple_of(NZ * ((c * NX + x) * NY + y), NZ), NZ), :]
                for c in range(NC)
            ]
            size = halves[0].shape[0]
            keep_ref[0, x, :size, :] = jnp.where(first, halves[0], halves[1])
            send_ref[0, x, :size, :] = jnp.where(first, halves[1], halves[0])
            keep_ref[0, x, size:, :] = jnp.where(first, extra[0], extra[1])
            send_ref[0, x, size:, :] = jnp.where(first, extra[1], extra[0])


def products(core, embeddings, matrix):
    rows, width = embeddings.shape
    rank = matrix.shape[1]
    wide = width // NY
    piece = wide // (NX * NC) + NZ
    blocks = jax.ShapeDtypeStruct((NY, NX, piece, rank), jnp.float32)
    spec = pl.BlockSpec((1, NX, piece, rank), lambda i: (jnp.maximum(i - NY, 0), 0, 0, 0))
    return pl.pallas_call(
        products_kernel,
        grid=(2 * NY,),
        out_shape=(jax.ShapeDtypeStruct((rows, rank), jnp.float32), blocks, blocks),
        in_specs=[
            pl.BlockSpec(memory_space=pltpu.SMEM),
            pl.BlockSpec((rows, wide), lambda i: (0, jnp.minimum(i, NY - 1))),
            pl.BlockSpec((wide, rank), lambda i: (jnp.minimum(i, NY - 1), 0)),
        ],
        out_specs=(pl.BlockSpec((rows, rank), lambda i: (0, 0)), spec, spec),
        scratch_shapes=[
            pltpu.VMEM((NY, rows, wide), jnp.bfloat16),
            pltpu.VMEM((NY, rows, wide), jnp.bfloat16),
            pltpu.VMEM((rank, rank), jnp.float32),
            pltpu.VMEM((rows, rank), jnp.bfloat16),
            pltpu.VMEM((rows, rank), jnp.bfloat16),
        ],
        compiler_params=pltpu.CompilerParams(vmem_limit_bytes=VMEM_LIMIT),
        cost_estimate=pl.CostEstimate(
            flops=12 * rows * width * rank, bytes_accessed=24 * 2**20, transcendentals=0
        ),
    )(core, embeddings, matrix)


def join(core_ref, mine_ref, other_ref, out_ref):
    half = mine_ref.shape[0]
    first = core_ref[0] == 0
    out_ref[:half, :] = jnp.where(first, mine_ref[...], other_ref[...])
    out_ref[half:, :] = jnp.where(first, other_ref[...], mine_ref[...])


def eliminate(out_ref, left, right):
    order = left.shape[0]
    sub = lax.broadcasted_iota(jnp.int32, (GROUP, LANES), 0)
    halves = order // LANES
    for start in range(0, order, PANEL):
        home = start // LANES
        rows = pl.ds(start, PANEL)
        left_at = list(range(home, halves))
        right_at = list(range(0, home + 1))
        tiles = [left[rows, pl.ds(h * LANES, LANES)] for h in left_at]
        tiles += [right[rows, pl.ds(h * LANES, LANES)] for h in right_at]
        done = [[] for _ in tiles]
        pivots = []
        for group in range(0, PANEL, GROUP):
            lane = start + group - home * LANES
            tall = tiles[0].shape[0]
            cols = [
                jnp.broadcast_to(tiles[0][:, lane + m : lane + m + 1], (tall, LANES))
                for m in range(GROUP)
            ]
            for j in range(GROUP):
                pivot = cols[j][j : j + 1, :]
                pivots.append(pivot)
                factor = cols[j] * (1.0 / pivot)
                top = jnp.where(sub > j, factor[:GROUP], 0.0)
                factor = top if tall == GROUP else jnp.concatenate([top, factor[GROUP:]], axis=0)
                tiles = [t - factor * t[j : j + 1, :] for t in tiles]
                cols = [
                    q if m <= j else q - factor * q[j : j + 1, :] for m, q in enumerate(cols)
                ]
            for i, t in enumerate(tiles):
                done[i].append(t[:GROUP])
            tiles = [t[GROUP:] for t in tiles]
        scale = lax.rsqrt(jnp.concatenate(pivots, axis=0))
        full = [jnp.concatenate(d, axis=0) * scale for d in done]
        for h, t in zip(right_at, full[len(left_at) :]):
            out_ref[rows, pl.ds(h * LANES, LANES)] = t
        below = start + PANEL
        for i, h in enumerate(left_at):
            first = max(below, h * LANES)
            if first >= (h + 1) * LANES:
                continue
            target = pl.ds(first, (h + 1) * LANES - first)
            flipped = full[i].T[first - h * LANES :]
            for k, g in enumerate(left_at):
                if g >= h:
                    left[target, pl.ds(g * LANES, LANES)] -= nn(flipped, full[k])
            for k, g in enumerate(right_at):
                right[target, pl.ds(g * LANES, LANES)] -= nn(flipped, full[len(left_at) + k])


def basis_kernel(
    scale, core_ref, mine_ref, other_ref, sketch_ref, rows_ref, inverse_ref, basis_ref, out_ref,
    left, right,
):
    order = left.shape[0]
    join(core_ref, mine_ref, other_ref, left)
    across = lax.broadcasted_iota(jnp.int32, (order, order), 1)
    down = lax.broadcasted_iota(jnp.int32, (order, order), 0)
    right[...] = jnp.where(across == down, 1.0, 0.0)
    inverse_ref[...] = jnp.zeros_like(inverse_ref)
    eliminate(inverse_ref, left, right)
    inverse = inverse_ref[...]
    basis_ref[...] = nt(sketch_ref[...], inverse) * scale
    out_ref[...] = nt(rows_ref[...], inverse)


def basis(core, mine, other, sketch, block_rows, scale):
    order = sketch.shape[1]
    return pl.pallas_call(
        functools.partial(basis_kernel, scale),
        out_shape=(
            jax.ShapeDtypeStruct((order, order), jnp.float32),
            jax.ShapeDtypeStruct(sketch.shape, jnp.float32),
            jax.ShapeDtypeStruct(block_rows.shape, jnp.float32),
        ),
        in_specs=[pl.BlockSpec(memory_space=pltpu.SMEM)]
        + [pl.BlockSpec(memory_space=pltpu.VMEM)] * 4,
        scratch_shapes=[pltpu.VMEM((order, order), jnp.float32)] * 2,
        cost_estimate=pl.CostEstimate(flops=10**10, bytes_accessed=2**21, transcendentals=0),
    )(core, mine, other, sketch, block_rows)


def whiten_kernel(width, core_ref, mine_ref, other_ref, inverse_ref, rows_ref, out_ref, inner):
    join(core_ref, mine_ref, other_ref, inner)
    inverse = inverse_ref[...]
    order = inverse.shape[0]
    across = lax.broadcasted_iota(jnp.int32, (order, order), 1)
    down = lax.broadcasted_iota(jnp.int32, (order, order), 0)
    diagonal = jnp.where(across == down, 1.5, 0.0)
    inverse = split(inverse)
    cross = three(split(three(inverse, split(inner[...]), NN)), inverse, NT)
    squares = jnp.sum(cross * cross, axis=0, keepdims=True)
    frob = jnp.sqrt(jnp.sum(squares, axis=1, keepdims=True))
    now = cross * (1.0 / frob)
    projected = rows_ref[...] * jnp.sqrt(width / frob)
    for step in range(PSTEPS):
        middle = split(diagonal - 0.5 * now)
        if step < PSTEPS - 1:
            now = three(split(three(middle, split(now), NN)), middle, NN)
        projected = three(split(projected), middle, NN)
    out_ref[...] = projected


def whiten(core, mine, other, inverse, block_rows, width):
    order = inverse.shape[0]
    return pl.pallas_call(
        functools.partial(whiten_kernel, width),
        out_shape=jax.ShapeDtypeStruct(block_rows.shape, jnp.float32),
        in_specs=[pl.BlockSpec(memory_space=pltpu.SMEM)]
        + [pl.BlockSpec(memory_space=pltpu.VMEM)] * 4,
        scratch_shapes=[pltpu.VMEM((order, order), jnp.float32)],
        cost_estimate=pl.CostEstimate(flops=10**10, bytes_accessed=2**20, transcendentals=0),
    )(core, mine, other, inverse, block_rows)


def to_core(block):
    return lax.ppermute(block, "c", [(0, 1), (1, 0)])


def along_x(block, flip):
    return lax.ppermute(block, "x", [(x, x ^ flip) for x in range(NX)])


def exchange(blocks, axes):
    return lax.all_to_all(blocks, axes, 0, 0, tiled=True)


def per_device(embeddings, sketch_matrix):
    rank = sketch_matrix.shape[1]
    width = embeddings.shape[1]
    share = width // (NX * NC * NY * NZ)
    total_rows = embeddings.shape[0] * NX * NC * NY * NZ
    chips = NX * NY * NZ
    x, c = lax.axis_index("x"), lax.axis_index("c")
    first_core = c == 0
    core = c.reshape(1).astype(jnp.int32)

    sketch, keep, send = products(core, embeddings, sketch_matrix)
    chip = (keep + to_core(send)).reshape(NY * NX, -1, rank)
    line = jnp.sum(exchange(chip, ("y", "x")), axis=0)
    size = NZ * share
    line = jnp.concatenate([line[:size].reshape(NZ, share, rank), line[size:][:, None]], axis=1)
    own = jnp.sum(exchange(line, "z"), axis=0)
    own_product, own_gram = own[:share], own[share:]

    from_core = to_core(own_product)
    pair = jnp.concatenate(
        [
            jnp.where(first_core, own_product, from_core),
            jnp.where(first_core, from_core, own_product),
        ]
    )
    around = jnp.stack([pair] + [along_x(pair, r) for r in (1, 2, 3)])
    block_rows = jnp.concatenate(
        [lax.dynamic_index_in_dim(around, x ^ r, 0, keepdims=False) for r in range(NX)]
    )

    half = jnp.where(first_core, pair[:, :chips], pair[:, chips:])
    inner = tn(half, pair)
    packet = jnp.concatenate([inner, jnp.broadcast_to(own_gram, inner.shape)], axis=1)
    packet = exchange(packet, CHIPS)
    gram = packet[:, rank:]
    inner_row = jnp.sum(packet[:, :rank], axis=0, keepdims=True)
    inner = exchange(jnp.broadcast_to(inner_row, inner.shape), CHIPS)

    inverse, left_basis, projected = basis(
        core, gram, to_core(gram), sketch, block_rows, math.sqrt(total_rows)
    )
    inner, inverse = lax.optimization_barrier((inner, inverse))
    right_basis = whiten(core, inner, to_core(inner), inverse, projected, width)
    return (left_basis, right_basis)


def solution(mesh):
    fine = Mesh(mesh.devices.reshape(NX, NC, NY, NZ), AXES)
    return jax.shard_map(
        per_device,
        mesh=fine,
        in_specs=(P(AXES, None), P()),
        out_specs=(P(AXES, None), P(("y", "z"), None)),
        check_vma=False,
    )
```

```python
import functools
import math

import jax
import jax.numpy as jnp
from jax import lax
from jax.experimental import pallas as pl
from jax.experimental.pallas import tpu as pltpu
from jax.sharding import Mesh
from jax.sharding import PartitionSpec as P

PSTEPS = 6
NX, NC, NY, NZ = 4, 2, 4, 8
AXES = ("x", "c", "y", "z")
CHIPS = ("x", "y", "z")
PANEL, GROUP, LANES = 32, 8, 128
HIGHEST = lax.Precision.HIGHEST
VMEM_LIMIT = 48 * 2**20
NN, TN, NT = ((1,), (0,)), ((0,), (0,)), ((1,), (1,))


def dot(a, b, dims, precision=None):
    return lax.dot_general(
        a, b, (dims, ((), ())), precision=precision, preferred_element_type=jnp.float32
    )


def nn(a, b):
    return dot(a, b, ((1,), (0,)), HIGHEST)


def tn(a, b):
    return dot(a, b, ((0,), (0,)), HIGHEST)


def nt(a, b):
    return dot(a, b, ((1,), (1,)), HIGHEST)


def split(value):
    high = value.astype(jnp.bfloat16)
    return high, (value - high.astype(jnp.float32)).astype(jnp.bfloat16)


def three(a, b, dims):
    return dot(a[0], b[0], dims) + (dot(a[0], b[1], dims) + dot(a[1], b[0], dims))


def products_kernel(
    slots_ref, emb_ref, matrix_ref, sketch_ref, keep_a, keep_b, send_a, send_b, high, low, gram,
    s_high, s_low,
):
    step = pl.program_id(0)
    rank = matrix_ref.shape[1]

    @pl.when(step < NY)
    def _():
        parts = split(emb_ref[...])
        high[step], low[step] = parts
        term = three(parts, split(matrix_ref[...]), NN)

        @pl.when(step == 0)
        def _():
            sketch_ref[...] = term

        @pl.when(step > 0)
        def _():
            sketch_ref[...] += term

    @pl.when(step == NY)
    def _():
        sketch = sketch_ref[...]
        s_high[...], s_low[...] = split(sketch)
        gram[...] = tn(sketch, sketch)

    @pl.when(step >= NY)
    def _():
        y = step - NY
        product = three((high[y], low[y]), (s_high[...], s_low[...]), TN)
        product = product.reshape(NZ, NX, NC, -1, rank)
        first = slots_ref[0] == 0
        for x in range(NX):
            halves = [product[:, x, c].reshape(-1, rank) for c in range(NC)]
            extra = [
                gram[pl.ds(pl.multiple_of(NZ * ((c * NX + x) * NY + y), NZ), NZ), :]
                for c in range(NC)
            ]
            size = halves[0].shape[0] // 2
            kept = jnp.where(first, halves[0], halves[1])
            sent = jnp.where(first, halves[1], halves[0])
            keep_x, send_x = slots_ref[1 + 2 * NY + x], slots_ref[1 + 2 * NY + NX + x]
            keep_a[0, keep_x, :size, :] = kept[:size]
            send_a[0, send_x, :size, :] = sent[:size]
            keep_a[0, keep_x, size:, :] = jnp.where(first, extra[0], extra[1])
            send_a[0, send_x, size:, :] = jnp.where(first, extra[1], extra[0])
            keep_b[keep_x, 0] = kept[size:]
            send_b[send_x, 0] = sent[size:]


def products(slots, embeddings, matrix):
    rows, width = embeddings.shape
    rank = matrix.shape[1]
    wide = width // NY
    piece = wide // (NX * NC * 2)
    part_a = jax.ShapeDtypeStruct((NY, NX, piece + NZ, rank), jnp.float32)
    part_b = jax.ShapeDtypeStruct((NX, NY, piece, rank), jnp.float32)

    def spec_a(base):
        return pl.BlockSpec(
            (1,) + part_a.shape[1:], lambda i, s: (s[base + jnp.maximum(i - NY, 0)], 0, 0, 0)
        )

    def spec_b(base):
        return pl.BlockSpec(
            (NX, 1) + part_b.shape[2:], lambda i, s: (0, s[base + jnp.maximum(i - NY, 0)], 0, 0)
        )

    return pl.pallas_call(
        products_kernel,
        grid_spec=pltpu.PrefetchScalarGridSpec(
            num_scalar_prefetch=1,
            grid=(2 * NY,),
            in_specs=[
                pl.BlockSpec((rows, wide), lambda i, s: (0, jnp.minimum(i, NY - 1))),
                pl.BlockSpec((wide, rank), lambda i, s: (jnp.minimum(i, NY - 1), 0)),
            ],
            out_specs=(
                pl.BlockSpec((rows, rank), lambda i, s: (0, 0)),
                spec_a(1),
                spec_b(1),
                spec_a(1 + NY),
                spec_b(1 + NY),
            ),
            scratch_shapes=[
                pltpu.VMEM((NY, rows, wide), jnp.bfloat16),
                pltpu.VMEM((NY, rows, wide), jnp.bfloat16),
                pltpu.VMEM((rank, rank), jnp.float32),
                pltpu.VMEM((rows, rank), jnp.bfloat16),
                pltpu.VMEM((rows, rank), jnp.bfloat16),
            ],
        ),
        out_shape=(
            jax.ShapeDtypeStruct((rows, rank), jnp.float32), part_a, part_b, part_a, part_b
        ),
        compiler_params=pltpu.CompilerParams(vmem_limit_bytes=VMEM_LIMIT),
        cost_estimate=pl.CostEstimate(
            flops=12 * rows * width * rank, bytes_accessed=24 * 2**20, transcendentals=0
        ),
    )(slots, embeddings, matrix)


def join(core_ref, mine_ref, other_ref, out_ref):
    half = mine_ref.shape[0]
    first = core_ref[0] == 0
    out_ref[:half, :] = jnp.where(first, mine_ref[...], other_ref[...])
    out_ref[half:, :] = jnp.where(first, other_ref[...], mine_ref[...])


def eliminate(out_ref, left, right):
    order = left.shape[0]
    sub = lax.broadcasted_iota(jnp.int32, (GROUP, LANES), 0)
    halves = order // LANES
    for start in range(0, order, PANEL):
        home = start // LANES
        rows = pl.ds(start, PANEL)
        left_at = list(range(home, halves))
        right_at = list(range(0, home + 1))
        tiles = [left[rows, pl.ds(h * LANES, LANES)] for h in left_at]
        tiles += [right[rows, pl.ds(h * LANES, LANES)] for h in right_at]
        done = [[] for _ in tiles]
        pivots = []
        for group in range(0, PANEL, GROUP):
            lane = start + group - home * LANES
            tall = tiles[0].shape[0]
            cols = [
                jnp.broadcast_to(tiles[0][:, lane + m : lane + m + 1], (tall, LANES))
                for m in range(GROUP)
            ]
            for j in range(GROUP):
                pivot = cols[j][j : j + 1, :]
                pivots.append(pivot)
                factor = cols[j] * (1.0 / pivot)
                top = jnp.where(sub > j, factor[:GROUP], 0.0)
                factor = top if tall == GROUP else jnp.concatenate([top, factor[GROUP:]], axis=0)
                tiles = [t - factor * t[j : j + 1, :] for t in tiles]
                cols = [
                    q if m <= j else q - factor * q[j : j + 1, :] for m, q in enumerate(cols)
                ]
            for i, t in enumerate(tiles):
                done[i].append(t[:GROUP])
            tiles = [t[GROUP:] for t in tiles]
        scale = lax.rsqrt(jnp.concatenate(pivots, axis=0))
        full = [jnp.concatenate(d, axis=0) * scale for d in done]
        for h, t in zip(right_at, full[len(left_at) :]):
            out_ref[rows, pl.ds(h * LANES, LANES)] = t
        below = start + PANEL
        for i, h in enumerate(left_at):
            first = max(below, h * LANES)
            if first >= (h + 1) * LANES:
                continue
            target = pl.ds(first, (h + 1) * LANES - first)
            flipped = full[i].T[first - h * LANES :]
            for k, g in enumerate(left_at):
                if g >= h:
                    left[target, pl.ds(g * LANES, LANES)] -= nn(flipped, full[k])
            for k, g in enumerate(right_at):
                right[target, pl.ds(g * LANES, LANES)] -= nn(flipped, full[len(left_at) + k])


def basis_kernel(
    scale, core_ref, mine_ref, other_ref, sketch_ref, rows_ref, inverse_ref, basis_ref, out_ref,
    left, right,
):
    order = left.shape[0]
    join(core_ref, mine_ref, other_ref, left)
    across = lax.broadcasted_iota(jnp.int32, (order, order), 1)
    down = lax.broadcasted_iota(jnp.int32, (order, order), 0)
    right[...] = jnp.where(across == down, 1.0, 0.0)
    inverse_ref[...] = jnp.zeros_like(inverse_ref)
    eliminate(inverse_ref, left, right)
    inverse = inverse_ref[...]
    basis_ref[...] = nt(sketch_ref[...], inverse) * scale
    out_ref[...] = nt(rows_ref[...], inverse)


def basis(core, mine, other, sketch, block_rows, scale):
    order = sketch.shape[1]
    return pl.pallas_call(
        functools.partial(basis_kernel, scale),
        out_shape=(
            jax.ShapeDtypeStruct((order, order), jnp.float32),
            jax.ShapeDtypeStruct(sketch.shape, jnp.float32),
            jax.ShapeDtypeStruct(block_rows.shape, jnp.float32),
        ),
        in_specs=[pl.BlockSpec(memory_space=pltpu.SMEM)]
        + [pl.BlockSpec(memory_space=pltpu.VMEM)] * 4,
        scratch_shapes=[pltpu.VMEM((order, order), jnp.float32)] * 2,
        cost_estimate=pl.CostEstimate(flops=10**10, bytes_accessed=2**21, transcendentals=0),
    )(core, mine, other, sketch, block_rows)


def whiten_kernel(width, core_ref, mine_ref, other_ref, inverse_ref, rows_ref, out_ref, inner):
    join(core_ref, mine_ref, other_ref, inner)
    inverse = inverse_ref[...]
    order = inverse.shape[0]
    across = lax.broadcasted_iota(jnp.int32, (order, order), 1)
    down = lax.broadcasted_iota(jnp.int32, (order, order), 0)
    diagonal = jnp.where(across == down, 1.5, 0.0)
    inverse = split(inverse)
    cross = three(split(three(inverse, split(inner[...]), NN)), inverse, NT)
    squares = jnp.sum(cross * cross, axis=0, keepdims=True)
    frob = jnp.sqrt(jnp.sum(squares, axis=1, keepdims=True))
    now = cross * (1.0 / frob)
    projected = rows_ref[...] * jnp.sqrt(width / frob)
    for step in range(PSTEPS):
        middle = split(diagonal - 0.5 * now)
        if step < PSTEPS - 1:
            now = three(split(three(middle, split(now), NN)), middle, NN)
        projected = three(split(projected), middle, NN)
    out_ref[...] = projected


def whiten(core, mine, other, inverse, block_rows, width):
    order = inverse.shape[0]
    return pl.pallas_call(
        functools.partial(whiten_kernel, width),
        out_shape=jax.ShapeDtypeStruct(block_rows.shape, jnp.float32),
        in_specs=[pl.BlockSpec(memory_space=pltpu.SMEM)]
        + [pl.BlockSpec(memory_space=pltpu.VMEM)] * 4,
        scratch_shapes=[pltpu.VMEM((order, order), jnp.float32)],
        cost_estimate=pl.CostEstimate(flops=10**10, bytes_accessed=2**20, transcendentals=0),
    )(core, mine, other, inverse, block_rows)


def to_core(block):
    return lax.ppermute(block, "c", [(0, 1), (1, 0)])


def along_x(block, flip):
    return lax.ppermute(block, "x", [(x, x ^ flip) for x in range(NX)])


def exchange(blocks, axes):
    return lax.all_to_all(blocks, axes, 0, 0, tiled=True)


def ring_pairs(block, axis, turn):
    pairs = []
    for c in range(NC):
        flip = 1 if turn == c else 3
        pairs += [(c * 4 + i, c * 4 + (i ^ flip)) for i in range(4)]
    if axis == "y":
        return lax.ppermute(block, ("c", "y"), pairs)
    pairs = [((i % 4) * NC + i // 4, (j % 4) * NC + j // 4) for i, j in pairs]
    return lax.ppermute(block, ("x", "c"), pairs)


def ring_slots(core, here):
    apart = jnp.arange(4, dtype=jnp.int32) ^ here
    return jnp.where((core == 1) & (apart % 2 == 1), 4 - apart, apart)


def ring_sums(terms_a, terms_b, axis_a, axis_b):
    def first(terms, slot):
        return functools.reduce(lambda p, q: p + q, [t[slot] for t in terms])

    out = []
    sent = [sum(t[1:3] for t in terms) for terms in (terms_a, terms_b)]
    got = [ring_pairs(v, axis, 0) for v, axis in zip(sent, (axis_a, axis_b))]
    got = lax.optimization_barrier(tuple(got))
    sent = [first(terms, 3) + g[1] for terms, g in zip((terms_a, terms_b), got)]
    more = [ring_pairs(v, axis, 1) for v, axis in zip(sent, (axis_a, axis_b))]
    more = lax.optimization_barrier(tuple(more))
    for terms, g, m in zip((terms_a, terms_b), got, more):
        out.append([first(terms, 0), g[0], m])
    return out


def per_device(embeddings, sketch_matrix):
    rank = sketch_matrix.shape[1]
    width = embeddings.shape[1]
    share = width // (NX * NC * NY * NZ)
    total_rows = embeddings.shape[0] * NX * NC * NY * NZ
    chips = NX * NY * NZ
    x, c, y = (lax.axis_index(name).astype(jnp.int32) for name in ("x", "c", "y"))
    first_core = c == 0
    core = c.reshape(1)

    slots = jnp.concatenate(
        [core] + [ring_slots(k, at) for at in (y, x) for k in (c, 1 - c)]
    )
    sketch, keep_a, keep_b, send_a, send_b = products(slots, embeddings, sketch_matrix)
    got_a, got_b = to_core(send_a), to_core(send_b)
    line_a, line_b = ring_sums([keep_a, got_a], [keep_b, got_b], "y", "x")
    own_a, own_b = ring_sums(line_a, line_b, "x", "y")
    own_a, own_b = sum(own_a), sum(own_b)
    size = own_b.shape[0]
    line = jnp.concatenate([own_a[:size], own_b]).reshape(NZ, share, rank)
    line = jnp.concatenate([line, own_a[size:][:, None]], axis=1)
    own = jnp.sum(exchange(line, "z"), axis=0)
    own_product, own_gram = own[:share], own[share:]

    from_core = to_core(own_product)
    pair = jnp.concatenate(
        [
            jnp.where(first_core, own_product, from_core),
            jnp.where(first_core, from_core, own_product),
        ]
    )
    around = jnp.stack([pair] + [along_x(pair, r) for r in (1, 2, 3)])
    block_rows = jnp.concatenate(
        [lax.dynamic_index_in_dim(around, x ^ r, 0, keepdims=False) for r in range(NX)]
    )

    half = jnp.where(first_core, pair[:, :chips], pair[:, chips:])
    inner = tn(half, pair)
    packet = jnp.concatenate([inner, jnp.broadcast_to(own_gram, inner.shape)], axis=1)
    packet = exchange(packet, CHIPS)
    gram = packet[:, rank:]
    inner_row = jnp.sum(packet[:, :rank], axis=0, keepdims=True)
    inner = exchange(jnp.broadcast_to(inner_row, inner.shape), CHIPS)

    inverse, left_basis, projected = basis(
        core, gram, to_core(gram), sketch, block_rows, math.sqrt(total_rows)
    )
    inner, inverse = lax.optimization_barrier((inner, inverse))
    right_basis = whiten(core, inner, to_core(inner), inverse, projected, width)
    return (left_basis, right_basis)


def solution(mesh):
    fine = Mesh(mesh.devices.reshape(NX, NC, NY, NZ), AXES)
    return jax.shard_map(
        per_device,
        mesh=fine,
        in_specs=(P(AXES, None), P()),
        out_specs=(P(AXES, None), P(("y", "z"), None)),
        check_vma=False,
    )
```

```python
import functools
import math

import jax
import jax.numpy as jnp
from jax import lax
from jax.experimental import pallas as pl
from jax.experimental.pallas import tpu as pltpu
from jax.sharding import Mesh
from jax.sharding import PartitionSpec as P

PSTEPS = 6
NX, NC, NY, NZ = 4, 2, 4, 8
LOADS = 2
AXES = ("x", "c", "y", "z")
CHIPS = ("x", "y", "z")
PANEL, GROUP, LANES = 64, 16, 128
HIGHEST = lax.Precision.HIGHEST
VMEM_LIMIT = 48 * 2**20
NN, TN, NT = ((1,), (0,)), ((0,), (0,)), ((1,), (1,))


def dot(a, b, dims, precision=None):
    return lax.dot_general(
        a, b, (dims, ((), ())), precision=precision, preferred_element_type=jnp.float32
    )


def nn(a, b):
    return dot(a, b, ((1,), (0,)), HIGHEST)


def tn(a, b):
    return dot(a, b, ((0,), (0,)), HIGHEST)


def nt(a, b):
    return dot(a, b, ((1,), (1,)), HIGHEST)


def split(value):
    high = value.astype(jnp.bfloat16)
    return high, (value - high.astype(jnp.float32)).astype(jnp.bfloat16)


def three(a, b, dims):
    return dot(a[0], b[0], dims) + (dot(a[0], b[1], dims) + dot(a[1], b[0], dims))


def products_kernel(
    slots_ref, emb_ref, matrix_ref, sketch_ref, keep_a, keep_b, send_a, send_b, high, low, gram,
    s_high, s_low,
):
    step = pl.program_id(0)
    rank = matrix_ref.shape[1]
    wide = high.shape[2]

    @pl.when(step < LOADS)
    def _():
        parts = split(emb_ref[...])
        for k in range(NY // LOADS):
            at = step * (NY // LOADS) + k
            high[at] = parts[0][:, k * wide : (k + 1) * wide]
            low[at] = parts[1][:, k * wide : (k + 1) * wide]
        term = three(parts, split(matrix_ref[...]), NN)

        @pl.when(step == 0)
        def _():
            sketch_ref[...] = term

        @pl.when(step > 0)
        def _():
            sketch_ref[...] += term

    @pl.when(step == LOADS)
    def _():
        sketch = sketch_ref[...]
        s_high[...], s_low[...] = split(sketch)
        gram[...] = tn(sketch, sketch)

    @pl.when(step >= LOADS)
    def _():
        y = step - LOADS
        product = three((high[y], low[y]), (s_high[...], s_low[...]), TN)
        product = product.reshape(NZ, NX, NC, -1, rank)
        first = slots_ref[0] == 0
        for x in range(NX):
            halves = [product[:, x, c].reshape(-1, rank) for c in range(NC)]
            extra = [
                gram[pl.ds(pl.multiple_of(NZ * ((c * NX + x) * NY + y), NZ), NZ), :]
                for c in range(NC)
            ]
            size = halves[0].shape[0] // 2
            kept = jnp.where(first, halves[0], halves[1])
            sent = jnp.where(first, halves[1], halves[0])
            keep_x, send_x = slots_ref[1 + 2 * NY + x], slots_ref[1 + 2 * NY + NX + x]
            keep_a[0, keep_x, :size, :] = kept[:size]
            send_a[0, send_x, :size, :] = sent[:size]
            keep_a[0, keep_x, size:, :] = jnp.where(first, extra[0], extra[1])
            send_a[0, send_x, size:, :] = jnp.where(first, extra[1], extra[0])
            keep_b[keep_x, 0] = kept[size:]
            send_b[send_x, 0] = sent[size:]


def products(slots, embeddings, matrix):
    rows, width = embeddings.shape
    rank = matrix.shape[1]
    wide = width // NY
    piece = wide // (NX * NC * 2)
    part_a = jax.ShapeDtypeStruct((NY, NX, piece + NZ, rank), jnp.float32)
    part_b = jax.ShapeDtypeStruct((NX, NY, piece, rank), jnp.float32)

    def spec_a(base):
        return pl.BlockSpec(
            (1,) + part_a.shape[1:], lambda i, s: (s[base + jnp.maximum(i - LOADS, 0)], 0, 0, 0)
        )

    def spec_b(base):
        return pl.BlockSpec(
            (NX, 1) + part_b.shape[2:], lambda i, s: (0, s[base + jnp.maximum(i - LOADS, 0)], 0, 0)
        )

    return pl.pallas_call(
        products_kernel,
        grid_spec=pltpu.PrefetchScalarGridSpec(
            num_scalar_prefetch=1,
            grid=(LOADS + NY,),
            in_specs=[
                pl.BlockSpec((rows, width // LOADS), lambda i, s: (0, jnp.minimum(i, LOADS - 1))),
                pl.BlockSpec((width // LOADS, rank), lambda i, s: (jnp.minimum(i, LOADS - 1), 0)),
            ],
            out_specs=(
                pl.BlockSpec((rows, rank), lambda i, s: (0, 0)),
                spec_a(1),
                spec_b(1),
                spec_a(1 + NY),
                spec_b(1 + NY),
            ),
            scratch_shapes=[
                pltpu.VMEM((NY, rows, wide), jnp.bfloat16),
                pltpu.VMEM((NY, rows, wide), jnp.bfloat16),
                pltpu.VMEM((rank, rank), jnp.float32),
                pltpu.VMEM((rows, rank), jnp.bfloat16),
                pltpu.VMEM((rows, rank), jnp.bfloat16),
            ],
        ),
        out_shape=(
            jax.ShapeDtypeStruct((rows, rank), jnp.float32), part_a, part_b, part_a, part_b
        ),
        compiler_params=pltpu.CompilerParams(vmem_limit_bytes=VMEM_LIMIT),
        cost_estimate=pl.CostEstimate(
            flops=12 * rows * width * rank, bytes_accessed=24 * 2**20, transcendentals=0
        ),
    )(slots, embeddings, matrix)


def join(core_ref, mine_ref, other_ref, out_ref):
    half = mine_ref.shape[0]
    first = core_ref[0] == 0
    out_ref[:half, :] = jnp.where(first, mine_ref[...], other_ref[...])
    out_ref[half:, :] = jnp.where(first, other_ref[...], mine_ref[...])


def eliminate(out_ref, left, right):
    order = left.shape[0]
    sub = lax.broadcasted_iota(jnp.int32, (GROUP, LANES), 0)
    halves = order // LANES
    for start in range(0, order, PANEL):
        home = start // LANES
        rows = pl.ds(start, PANEL)
        left_at = list(range(home, halves))
        right_at = list(range(0, home + 1))
        tiles = [left[rows, pl.ds(h * LANES, LANES)] for h in left_at]
        tiles += [right[rows, pl.ds(h * LANES, LANES)] for h in right_at]
        done = [[] for _ in tiles]
        pivots = []
        for group in range(0, PANEL, GROUP):
            lane = start + group - home * LANES
            tall = tiles[0].shape[0]
            cols = [
                jnp.broadcast_to(tiles[0][:, lane + m : lane + m + 1], (tall, LANES))
                for m in range(GROUP)
            ]
            for j in range(GROUP):
                pivot = cols[j][j : j + 1, :]
                pivots.append(pivot)
                low = jnp.where(sub > j, cols[j][:GROUP], 0.0)
                if tall > GROUP:
                    low = jnp.concatenate([low, cols[j][GROUP:]], axis=0)
                pivot = 1.0 / pivot
                tiles = [t - low * (t[j : j + 1, :] * pivot) for t in tiles]
                cols = [
                    q if m <= j else q - low * (q[j : j + 1, :] * pivot) for m, q in enumerate(cols)
                ]
            for i, t in enumerate(tiles):
                done[i].append(t[:GROUP])
            tiles = [t[GROUP:] for t in tiles]
        scale = lax.rsqrt(jnp.concatenate(pivots, axis=0))
        full = [jnp.concatenate(d, axis=0) * scale for d in done]
        for h, t in zip(right_at, full[len(left_at) :]):
            out_ref[rows, pl.ds(h * LANES, LANES)] = t
        below = start + PANEL
        for i, h in enumerate(left_at):
            first = max(below, h * LANES)
            if first >= (h + 1) * LANES:
                continue
            target = pl.ds(first, (h + 1) * LANES - first)
            flipped = full[i].T[first - h * LANES :]
            for k, g in enumerate(left_at):
                if g >= h:
                    left[target, pl.ds(g * LANES, LANES)] -= nn(flipped, full[k])
            for k, g in enumerate(right_at):
                right[target, pl.ds(g * LANES, LANES)] -= nn(flipped, full[len(left_at) + k])


def basis_kernel(
    scale, slots_ref, mine_ref, other_ref, sketch_ref, part_0, part_1, part_2, part_3, inverse_ref,
    basis_ref, out_ref, left, right, rows,
):
    order = left.shape[0]
    join(slots_ref, mine_ref, other_ref, left)
    for r, part in enumerate((part_0, part_1, part_2, part_3)):
        size = part.shape[0]
        at = pl.multiple_of((slots_ref[slots_ref.shape[0] - 1] ^ r) * size, size)
        rows[pl.ds(at, size), :] = part[...]
    across = lax.broadcasted_iota(jnp.int32, (order, order), 1)
    down = lax.broadcasted_iota(jnp.int32, (order, order), 0)
    right[...] = jnp.where(across == down, 1.0, 0.0)
    inverse_ref[...] = jnp.zeros_like(inverse_ref)
    eliminate(inverse_ref, left, right)
    inverse = split(inverse_ref[...])
    basis_ref[...] = three(split(sketch_ref[...]), inverse, NT) * scale
    out_ref[...] = three(split(rows[...]), inverse, NT)


def basis(slots, mine, other, sketch, parts, scale):
    order = sketch.shape[1]
    rows = jax.ShapeDtypeStruct((NX * parts[0].shape[0], order), jnp.float32)
    return pl.pallas_call(
        functools.partial(basis_kernel, scale),
        out_shape=(
            jax.ShapeDtypeStruct((order, order), jnp.float32),
            jax.ShapeDtypeStruct(sketch.shape, jnp.float32),
            rows,
        ),
        in_specs=[pl.BlockSpec(memory_space=pltpu.SMEM)]
        + [pl.BlockSpec(memory_space=pltpu.VMEM)] * (3 + NX),
        scratch_shapes=[pltpu.VMEM((order, order), jnp.float32)] * 2
        + [pltpu.VMEM(rows.shape, jnp.float32)],
        cost_estimate=pl.CostEstimate(flops=10**10, bytes_accessed=2**21, transcendentals=0),
    )(slots, mine, other, sketch, *parts)


def whiten_kernel(width, slots_ref, mine_ref, other_ref, inverse_ref, rows_ref, out_ref, inner):
    join(slots_ref, mine_ref, other_ref, inner)
    inverse = split(inverse_ref[...])
    order = inverse_ref.shape[0]
    across = lax.broadcasted_iota(jnp.int32, (order, order), 1)
    down = lax.broadcasted_iota(jnp.int32, (order, order), 0)
    diagonal = jnp.where(across == down, 1.5, 0.0)
    cross = three(split(three(inverse, split(inner[...]), NN)), inverse, NT)
    squares = jnp.sum(cross * cross, axis=0, keepdims=True)
    frob = jnp.sqrt(jnp.sum(squares, axis=1, keepdims=True))
    now = cross * (1.0 / frob)
    projected = rows_ref[...] * jnp.sqrt(width / frob)
    for step in range(PSTEPS):
        middle = split(diagonal - 0.5 * now)
        if step < PSTEPS - 1:
            halves = [now[:LANES], now[LANES:]]
            for _ in range(2):
                halves = [three(split(half), middle, NN) for half in halves]
            now = jnp.concatenate(halves, axis=0)
        projected = three(split(projected), middle, NN)
    out_ref[...] = projected


def whiten(slots, mine, other, inverse, block_rows, width):
    order = inverse.shape[0]
    return pl.pallas_call(
        functools.partial(whiten_kernel, width),
        out_shape=jax.ShapeDtypeStruct(block_rows.shape, jnp.float32),
        in_specs=[pl.BlockSpec(memory_space=pltpu.SMEM)]
        + [pl.BlockSpec(memory_space=pltpu.VMEM)] * 4,
        scratch_shapes=[pltpu.VMEM((order, order), jnp.float32)],
        cost_estimate=pl.CostEstimate(flops=10**10, bytes_accessed=2**20, transcendentals=0),
    )(slots, mine, other, inverse, block_rows)


def to_core(block):
    return lax.ppermute(block, "c", [(0, 1), (1, 0)])


def along_x(block, flip):
    return lax.ppermute(block, "x", [(x, x ^ flip) for x in range(NX)])


def exchange(blocks, axes):
    return lax.all_to_all(blocks, axes, 0, 0, tiled=True)


def ring_pairs(block, axis, turn):
    pairs = []
    for c in range(NC):
        flip = 1 if turn == c else 3
        pairs += [(c * 4 + i, c * 4 + (i ^ flip)) for i in range(4)]
    if axis == "y":
        return lax.ppermute(block, ("c", "y"), pairs)
    pairs = [((i % 4) * NC + i // 4, (j % 4) * NC + j // 4) for i, j in pairs]
    return lax.ppermute(block, ("x", "c"), pairs)


def ring_slots(core, here):
    apart = jnp.arange(4, dtype=jnp.int32) ^ here
    return jnp.where((core == 1) & (apart % 2 == 1), 4 - apart, apart)


def ring_sums(terms_a, terms_b, axis_a, axis_b):
    def first(terms, slot):
        return functools.reduce(lambda p, q: p + q, [t[slot] for t in terms])

    out = []
    sent = [sum(t[1:3] for t in terms) for terms in (terms_a, terms_b)]
    got = [ring_pairs(v, axis, 0) for v, axis in zip(sent, (axis_a, axis_b))]
    got = lax.optimization_barrier(tuple(got))
    sent = [first(terms, 3) + g[1] for terms, g in zip((terms_a, terms_b), got)]
    more = [ring_pairs(v, axis, 1) for v, axis in zip(sent, (axis_a, axis_b))]
    more = lax.optimization_barrier(tuple(more))
    for terms, g, m in zip((terms_a, terms_b), got, more):
        out.append([first(terms, 0), g[0], m])
    return out


def per_device(embeddings, sketch_matrix):
    rank = sketch_matrix.shape[1]
    width = embeddings.shape[1]
    share = width // (NX * NC * NY * NZ)
    total_rows = embeddings.shape[0] * NX * NC * NY * NZ
    chips = NX * NY * NZ
    x, c, y = (lax.axis_index(name).astype(jnp.int32) for name in ("x", "c", "y"))
    first_core = c == 0
    core = c.reshape(1)

    slots = jnp.concatenate(
        [core] + [ring_slots(k, at) for at in (y, x) for k in (c, 1 - c)] + [x.reshape(1)]
    )
    sketch, keep_a, keep_b, send_a, send_b = products(slots, embeddings, sketch_matrix)
    got_a, got_b = to_core(send_a), to_core(send_b)
    line_a, line_b = ring_sums([keep_a, got_a], [keep_b, got_b], "y", "x")
    own_a, own_b = ring_sums(line_a, line_b, "x", "y")
    own_a, own_b = sum(own_a), sum(own_b)
    size = own_b.shape[0]
    line = jnp.concatenate([own_a[:size], own_b]).reshape(NZ, share, rank)
    line = jnp.concatenate([line, own_a[size:][:, None]], axis=1)
    own = jnp.sum(exchange(line, "z"), axis=0)
    own_product, own_gram = own[:share], own[share:]

    from_core = to_core(own_product)
    pair = jnp.concatenate(
        [
            jnp.where(first_core, own_product, from_core),
            jnp.where(first_core, from_core, own_product),
        ]
    )
    half = jnp.where(first_core, pair[:, :chips], pair[:, chips:])
    inner = tn(half, pair)
    packet = jnp.concatenate([inner, jnp.broadcast_to(own_gram, inner.shape)], axis=1)
    packet, *parts = lax.optimization_barrier(
        (exchange(packet, CHIPS), pair, *(along_x(pair, r) for r in (1, 2, 3)))
    )
    gram = packet[:, rank:]
    inner_row = jnp.sum(packet[:, :rank], axis=0, keepdims=True)
    inner = exchange(jnp.broadcast_to(inner_row, inner.shape), CHIPS)
    inverse, left_basis, projected = basis(
        slots, gram, to_core(gram), sketch, parts, math.sqrt(total_rows)
    )
    inner, inverse = lax.optimization_barrier((inner, inverse))
    right_basis = whiten(slots, inner, to_core(inner), inverse, projected, width)
    return (left_basis, right_basis)


def solution(mesh):
    fine = Mesh(mesh.devices.reshape(NX, NC, NY, NZ), AXES)
    return jax.shard_map(
        per_device,
        mesh=fine,
        in_specs=(P(AXES, None), P()),
        out_specs=(P(AXES, None), P(("y", "z"), None)),
        check_vma=False,
    )
```

```python
import functools
import math

import jax
import jax.numpy as jnp
from jax import lax
from jax.experimental import pallas as pl
from jax.experimental.pallas import tpu as pltpu
from jax.sharding import Mesh
from jax.sharding import PartitionSpec as P

PSTEPS = 6
NX, NC, NY, NZ = 4, 2, 4, 8
LOADS = 2
AXES = ("x", "c", "y", "z")
CHIPS = ("x", "y", "z")
PANEL, GROUP, LANES = 64, 16, 128
HIGHEST = lax.Precision.HIGHEST
VMEM_LIMIT = 48 * 2**20
SMALL_LIMIT = 16 * 2**20
NN, TN, NT = ((1,), (0,)), ((0,), (0,)), ((1,), (1,))


def dot(a, b, dims, precision=None):
    return lax.dot_general(
        a, b, (dims, ((), ())), precision=precision, preferred_element_type=jnp.float32
    )


def nn(a, b):
    return dot(a, b, ((1,), (0,)), HIGHEST)


def tn(a, b):
    return dot(a, b, ((0,), (0,)), HIGHEST)


def nt(a, b):
    return dot(a, b, ((1,), (1,)), HIGHEST)


def split(value):
    high = value.astype(jnp.bfloat16)
    return high, (value - high.astype(jnp.float32)).astype(jnp.bfloat16)


def three(a, b, dims):
    return dot(a[0], b[0], dims) + (dot(a[0], b[1], dims) + dot(a[1], b[0], dims))


def products_kernel(
    slots_ref, emb_ref, matrix_ref, sketch_ref, keep_a, keep_b, send_a, send_b, high, low, gram,
    s_high, s_low,
):
    step = pl.program_id(0)
    rank = matrix_ref.shape[1]
    wide = high.shape[2]

    @pl.when(step < LOADS)
    def _():
        parts = split(emb_ref[...])
        for k in range(NY // LOADS):
            at = step * (NY // LOADS) + k
            high[at] = parts[0][:, k * wide : (k + 1) * wide]
            low[at] = parts[1][:, k * wide : (k + 1) * wide]
        term = three(parts, split(matrix_ref[...]), NN)

        @pl.when(step == 0)
        def _():
            sketch_ref[...] = term

        @pl.when(step > 0)
        def _():
            sketch_ref[...] += term

    @pl.when(step == LOADS)
    def _():
        sketch = sketch_ref[...]
        s_high[...], s_low[...] = split(sketch)
        gram[...] = tn(sketch, sketch)

    @pl.when(step >= LOADS)
    def _():
        y = step - LOADS
        product = three((high[y], low[y]), (s_high[...], s_low[...]), TN)
        product = product.reshape(NZ, NX, NC, -1, rank)
        first = slots_ref[0] == 0
        for x in range(NX):
            halves = [product[:, x, c].reshape(-1, rank) for c in range(NC)]
            extra = [
                gram[pl.ds(pl.multiple_of(NZ * ((c * NX + x) * NY + y), NZ), NZ), :]
                for c in range(NC)
            ]
            size = halves[0].shape[0] // 2
            kept = jnp.where(first, halves[0], halves[1])
            sent = jnp.where(first, halves[1], halves[0])
            keep_x, send_x = slots_ref[1 + 2 * NY + x], slots_ref[1 + 2 * NY + NX + x]
            keep_a[0, keep_x, :size, :] = kept[:size]
            send_a[0, send_x, :size, :] = sent[:size]
            keep_a[0, keep_x, size:, :] = jnp.where(first, extra[0], extra[1])
            send_a[0, send_x, size:, :] = jnp.where(first, extra[1], extra[0])
            keep_b[keep_x, 0] = kept[size:]
            send_b[send_x, 0] = sent[size:]


def products(slots, embeddings, matrix):
    rows, width = embeddings.shape
    rank = matrix.shape[1]
    wide = width // NY
    piece = wide // (NX * NC * 2)
    part_a = jax.ShapeDtypeStruct((NY, NX, piece + NZ, rank), jnp.float32)
    part_b = jax.ShapeDtypeStruct((NX, NY, piece, rank), jnp.float32)

    def spec_a(base):
        return pl.BlockSpec(
            (1,) + part_a.shape[1:], lambda i, s: (s[base + jnp.maximum(i - LOADS, 0)], 0, 0, 0)
        )

    def spec_b(base):
        return pl.BlockSpec(
            (NX, 1) + part_b.shape[2:], lambda i, s: (0, s[base + jnp.maximum(i - LOADS, 0)], 0, 0)
        )

    return pl.pallas_call(
        products_kernel,
        grid_spec=pltpu.PrefetchScalarGridSpec(
            num_scalar_prefetch=1,
            grid=(LOADS + NY,),
            in_specs=[
                pl.BlockSpec((rows, width // LOADS), lambda i, s: (0, jnp.minimum(i, LOADS - 1))),
                pl.BlockSpec((width // LOADS, rank), lambda i, s: (jnp.minimum(i, LOADS - 1), 0)),
            ],
            out_specs=(
                pl.BlockSpec((rows, rank), lambda i, s: (0, 0)),
                spec_a(1),
                spec_b(1),
                spec_a(1 + NY),
                spec_b(1 + NY),
            ),
            scratch_shapes=[
                pltpu.VMEM((NY, rows, wide), jnp.bfloat16),
                pltpu.VMEM((NY, rows, wide), jnp.bfloat16),
                pltpu.VMEM((rank, rank), jnp.float32),
                pltpu.VMEM((rows, rank), jnp.bfloat16),
                pltpu.VMEM((rows, rank), jnp.bfloat16),
            ],
        ),
        out_shape=(
            jax.ShapeDtypeStruct((rows, rank), jnp.float32), part_a, part_b, part_a, part_b
        ),
        compiler_params=pltpu.CompilerParams(vmem_limit_bytes=VMEM_LIMIT),
        cost_estimate=pl.CostEstimate(
            flops=12 * rows * width * rank, bytes_accessed=24 * 2**20, transcendentals=0
        ),
    )(slots, embeddings, matrix)


def join(core_ref, mine_ref, other_ref, out_ref):
    half = mine_ref.shape[0]
    first = core_ref[0] == 0
    out_ref[:half, :] = jnp.where(first, mine_ref[...], other_ref[...])
    out_ref[half:, :] = jnp.where(first, other_ref[...], mine_ref[...])


def eliminate(out_ref, left, right):
    order = left.shape[0]
    sub = lax.broadcasted_iota(jnp.int32, (GROUP, LANES), 0)
    halves = order // LANES
    for start in range(0, order, PANEL):
        home = start // LANES
        rows = pl.ds(start, PANEL)
        left_at = list(range(home, halves))
        right_at = list(range(0, home + 1))
        tiles = [left[rows, pl.ds(h * LANES, LANES)] for h in left_at]
        tiles += [right[rows, pl.ds(h * LANES, LANES)] for h in right_at]
        done = [[] for _ in tiles]
        pivots = []
        for group in range(0, PANEL, GROUP):
            lane = start + group - home * LANES
            tall = tiles[0].shape[0]
            cols = [
                jnp.broadcast_to(tiles[0][:, lane + m : lane + m + 1], (tall, LANES))
                for m in range(GROUP)
            ]
            for j in range(GROUP):
                pivot = cols[j][j : j + 1, :]
                pivots.append(pivot)
                low = jnp.where(sub > j, cols[j][:GROUP], 0.0)
                if tall > GROUP:
                    low = jnp.concatenate([low, cols[j][GROUP:]], axis=0)
                pivot = 1.0 / pivot
                tiles = [t - low * (t[j : j + 1, :] * pivot) for t in tiles]
                cols = [
                    q if m <= j else q - low * (q[j : j + 1, :] * pivot) for m, q in enumerate(cols)
                ]
            for i, t in enumerate(tiles):
                done[i].append(t[:GROUP])
            tiles = [t[GROUP:] for t in tiles]
        scale = lax.rsqrt(jnp.concatenate(pivots, axis=0))
        full = [jnp.concatenate(d, axis=0) * scale for d in done]
        for h, t in zip(right_at, full[len(left_at) :]):
            out_ref[rows, pl.ds(h * LANES, LANES)] = t
        below = start + PANEL
        for i, h in enumerate(left_at):
            first = max(below, h * LANES)
            if first >= (h + 1) * LANES:
                continue
            target = pl.ds(first, (h + 1) * LANES - first)
            flipped = full[i].T[first - h * LANES :]
            for k, g in enumerate(left_at):
                if g >= h:
                    left[target, pl.ds(g * LANES, LANES)] -= nn(flipped, full[k])
            for k, g in enumerate(right_at):
                right[target, pl.ds(g * LANES, LANES)] -= nn(flipped, full[len(left_at) + k])


def basis_kernel(
    scale, slots_ref, mine_ref, other_ref, sketch_ref, part_0, part_1, part_2, part_3, inverse_ref,
    basis_ref, out_ref, left, right, rows,
):
    order = left.shape[0]
    join(slots_ref, mine_ref, other_ref, left)
    for r, part in enumerate((part_0, part_1, part_2, part_3)):
        size = part.shape[0]
        at = pl.multiple_of((slots_ref[slots_ref.shape[0] - 1] ^ r) * size, size)
        rows[pl.ds(at, size), :] = part[...]
    across = lax.broadcasted_iota(jnp.int32, (order, order), 1)
    down = lax.broadcasted_iota(jnp.int32, (order, order), 0)
    right[...] = jnp.where(across == down, 1.0, 0.0)
    inverse_ref[...] = jnp.zeros_like(inverse_ref)
    eliminate(inverse_ref, left, right)
    inverse = split(inverse_ref[...])
    basis_ref[...] = three(split(sketch_ref[...]), inverse, NT) * scale
    out_ref[...] = three(split(rows[...]), inverse, NT)


def basis(slots, mine, other, sketch, parts, scale):
    order = sketch.shape[1]
    rows = jax.ShapeDtypeStruct((NX * parts[0].shape[0], order), jnp.float32)
    return pl.pallas_call(
        functools.partial(basis_kernel, scale),
        out_shape=(
            jax.ShapeDtypeStruct((order, order), jnp.float32),
            jax.ShapeDtypeStruct(sketch.shape, jnp.float32),
            rows,
        ),
        in_specs=[pl.BlockSpec(memory_space=pltpu.SMEM)]
        + [pl.BlockSpec(memory_space=pltpu.VMEM)] * (3 + NX),
        scratch_shapes=[pltpu.VMEM((order, order), jnp.float32)] * 2
        + [pltpu.VMEM(rows.shape, jnp.float32)],
        compiler_params=pltpu.CompilerParams(vmem_limit_bytes=SMALL_LIMIT),
        cost_estimate=pl.CostEstimate(flops=10**10, bytes_accessed=2**21, transcendentals=0),
    )(slots, mine, other, sketch, *parts)


def whiten_kernel(width, slots_ref, mine_ref, other_ref, inverse_ref, rows_ref, out_ref, inner):
    join(slots_ref, mine_ref, other_ref, inner)
    inverse = split(inverse_ref[...])
    order = inverse_ref.shape[0]
    across = lax.broadcasted_iota(jnp.int32, (order, order), 1)
    down = lax.broadcasted_iota(jnp.int32, (order, order), 0)
    diagonal = jnp.where(across == down, 1.5, 0.0)
    cross = three(split(three(inverse, split(inner[...]), NN)), inverse, NT)
    squares = jnp.sum(cross * cross, axis=0, keepdims=True)
    frob = jnp.sqrt(jnp.sum(squares, axis=1, keepdims=True))
    now = cross * (1.0 / frob)
    projected = rows_ref[...] * jnp.sqrt(width / frob)
    for step in range(PSTEPS):
        middle = split(diagonal - 0.5 * now)
        if step < PSTEPS - 1:
            halves = [now[:LANES], now[LANES:]]
            for _ in range(2):
                halves = [three(split(half), middle, NN) for half in halves]
            now = jnp.concatenate(halves, axis=0)
        projected = three(split(projected), middle, NN)
    out_ref[...] = projected


def whiten(slots, mine, other, inverse, block_rows, width):
    order = inverse.shape[0]
    return pl.pallas_call(
        functools.partial(whiten_kernel, width),
        out_shape=jax.ShapeDtypeStruct(block_rows.shape, jnp.float32),
        in_specs=[pl.BlockSpec(memory_space=pltpu.SMEM)]
        + [pl.BlockSpec(memory_space=pltpu.VMEM)] * 4,
        scratch_shapes=[pltpu.VMEM((order, order), jnp.float32)],
        compiler_params=pltpu.CompilerParams(vmem_limit_bytes=SMALL_LIMIT),
        cost_estimate=pl.CostEstimate(flops=10**10, bytes_accessed=2**20, transcendentals=0),
    )(slots, mine, other, inverse, block_rows)


def to_core(block):
    return lax.ppermute(block, "c", [(0, 1), (1, 0)])


def along_x(block, flip):
    return lax.ppermute(block, "x", [(x, x ^ flip) for x in range(NX)])


def exchange(blocks, axes):
    return lax.all_to_all(blocks, axes, 0, 0, tiled=True)


def ring_pairs(block, axis, turn):
    pairs = []
    for c in range(NC):
        flip = 1 if turn == c else 3
        pairs += [(c * 4 + i, c * 4 + (i ^ flip)) for i in range(4)]
    if axis == "y":
        return lax.ppermute(block, ("c", "y"), pairs)
    pairs = [((i % 4) * NC + i // 4, (j % 4) * NC + j // 4) for i, j in pairs]
    return lax.ppermute(block, ("x", "c"), pairs)


def ring_slots(core, here):
    apart = jnp.arange(4, dtype=jnp.int32) ^ here
    return jnp.where((core == 1) & (apart % 2 == 1), 4 - apart, apart)


def ring_sums(terms_a, terms_b, axis_a, axis_b):
    def first(terms, slot):
        return functools.reduce(lambda p, q: p + q, [t[slot] for t in terms])

    out = []
    sent = [sum(t[1:3] for t in terms) for terms in (terms_a, terms_b)]
    got = [ring_pairs(v, axis, 0) for v, axis in zip(sent, (axis_a, axis_b))]
    got = lax.optimization_barrier(tuple(got))
    sent = [first(terms, 3) + g[1] for terms, g in zip((terms_a, terms_b), got)]
    more = [ring_pairs(v, axis, 1) for v, axis in zip(sent, (axis_a, axis_b))]
    more = lax.optimization_barrier(tuple(more))
    for terms, g, m in zip((terms_a, terms_b), got, more):
        out.append([first(terms, 0), g[0], m])
    return out


def per_device(embeddings, sketch_matrix):
    rank = sketch_matrix.shape[1]
    width = embeddings.shape[1]
    share = width // (NX * NC * NY * NZ)
    total_rows = embeddings.shape[0] * NX * NC * NY * NZ
    chips = NX * NY * NZ
    x, c, y = (lax.axis_index(name).astype(jnp.int32) for name in ("x", "c", "y"))
    first_core = c == 0
    core = c.reshape(1)

    slots = jnp.concatenate(
        [core] + [ring_slots(k, at) for at in (y, x) for k in (c, 1 - c)] + [x.reshape(1)]
    )
    sketch, keep_a, keep_b, send_a, send_b = products(slots, embeddings, sketch_matrix)
    got_a, got_b = to_core(send_a), to_core(send_b)
    line_a, line_b = ring_sums([keep_a, got_a], [keep_b, got_b], "y", "x")
    own_a, own_b = ring_sums(line_a, line_b, "x", "y")
    own_a, own_b = sum(own_a), sum(own_b)
    size = own_b.shape[0]
    line = jnp.concatenate([own_a[:size], own_b]).reshape(NZ, share, rank)
    line = jnp.concatenate([line, own_a[size:][:, None]], axis=1)
    own = jnp.sum(exchange(line, "z"), axis=0)
    own_product, own_gram = own[:share], own[share:]

    from_core = to_core(own_product)
    pair = jnp.concatenate(
        [
            jnp.where(first_core, own_product, from_core),
            jnp.where(first_core, from_core, own_product),
        ]
    )
    half = jnp.where(first_core, pair[:, :chips], pair[:, chips:])
    inner = tn(half, pair)
    packet = jnp.concatenate([inner, jnp.broadcast_to(own_gram, inner.shape)], axis=1)
    packet, *parts = lax.optimization_barrier(
        (exchange(packet, CHIPS), pair, *(along_x(pair, r) for r in (1, 2, 3)))
    )
    gram = packet[:, rank:]
    inner_row = jnp.sum(packet[:, :rank], axis=0, keepdims=True)
    inner = exchange(jnp.broadcast_to(inner_row, inner.shape), CHIPS)
    inverse, left_basis, projected = basis(
        slots, gram, to_core(gram), sketch, parts, math.sqrt(total_rows)
    )
    inner, inverse = lax.optimization_barrier((inner, inverse))
    right_basis = whiten(slots, inner, to_core(inner), inverse, projected, width)
    return (left_basis, right_basis)


def solution(mesh):
    fine = Mesh(mesh.devices.reshape(NX, NC, NY, NZ), AXES)
    return jax.shard_map(
        per_device,
        mesh=fine,
        in_specs=(P(AXES, None), P()),
        out_specs=(P(AXES, None), P(("y", "z"), None)),
        check_vma=False,
    )
```

```python
import functools
import math

import jax
import jax.numpy as jnp
from jax import lax
from jax.experimental import pallas as pl
from jax.experimental.pallas import tpu as pltpu
from jax.sharding import Mesh
from jax.sharding import PartitionSpec as P

PSTEPS = 6
NX, NC, NY, NZ = 4, 2, 4, 8
LOADS = 2
AXES = ("x", "c", "y", "z")
CHIPS = ("x", "y", "z")
PANEL, GROUP, LANES = 64, 16, 128
HIGHEST = lax.Precision.HIGHEST
VMEM_LIMIT = 48 * 2**20
SMALL_LIMIT = 16 * 2**20
NN, TN, NT = ((1,), (0,)), ((0,), (0,)), ((1,), (1,))


def dot(a, b, dims, precision=None):
    return lax.dot_general(
        a, b, (dims, ((), ())), precision=precision, preferred_element_type=jnp.float32
    )


def nn(a, b):
    return dot(a, b, ((1,), (0,)), HIGHEST)


def tn(a, b):
    return dot(a, b, ((0,), (0,)), HIGHEST)


def nt(a, b):
    return dot(a, b, ((1,), (1,)), HIGHEST)


def split(value):
    high = value.astype(jnp.bfloat16)
    return high, (value - high.astype(jnp.float32)).astype(jnp.bfloat16)


def three(a, b, dims):
    return dot(a[0], b[0], dims) + (dot(a[0], b[1], dims) + dot(a[1], b[0], dims))


def products_kernel(
    slots_ref, emb_ref, matrix_ref, sketch_ref, keep_a, keep_b, send_a, send_b, high, low, gram,
    s_high, s_low,
):
    step = pl.program_id(0)
    rank = matrix_ref.shape[1]
    wide = high.shape[2]

    @pl.when(step < LOADS)
    def _():
        parts = split(emb_ref[...])
        for k in range(NY // LOADS):
            at = step * (NY // LOADS) + k
            high[at] = parts[0][:, k * wide : (k + 1) * wide]
            low[at] = parts[1][:, k * wide : (k + 1) * wide]
        term = three(parts, split(matrix_ref[...]), NN)

        @pl.when(step == 0)
        def _():
            sketch_ref[...] = term

        @pl.when(step > 0)
        def _():
            sketch_ref[...] += term

    @pl.when(step == LOADS)
    def _():
        sketch = sketch_ref[...]
        s_high[...], s_low[...] = split(sketch)
        gram[...] = tn(sketch, sketch)

    @pl.when(step >= LOADS)
    def _():
        y = step - LOADS
        product = three((high[y], low[y]), (s_high[...], s_low[...]), TN)
        product = product.reshape(NZ, NX, NC, -1, rank)
        first = slots_ref[0] == 0
        for x in range(NX):
            halves = [product[:, x, c].reshape(-1, rank) for c in range(NC)]
            extra = [
                gram[pl.ds(pl.multiple_of(NZ * ((c * NX + x) * NY + y), NZ), NZ), :]
                for c in range(NC)
            ]
            size = halves[0].shape[0] // 2
            kept = jnp.where(first, halves[0], halves[1])
            sent = jnp.where(first, halves[1], halves[0])
            keep_x, send_x = slots_ref[1 + 2 * NY + x], slots_ref[1 + 2 * NY + NX + x]
            keep_a[0, keep_x, :size, :] = kept[:size]
            send_a[0, send_x, :size, :] = sent[:size]
            keep_a[0, keep_x, size:, :] = jnp.where(first, extra[0], extra[1])
            send_a[0, send_x, size:, :] = jnp.where(first, extra[1], extra[0])
            keep_b[keep_x, 0] = kept[size:]
            send_b[send_x, 0] = sent[size:]


def products(slots, embeddings, matrix):
    rows, width = embeddings.shape
    rank = matrix.shape[1]
    wide = width // NY
    piece = wide // (NX * NC * 2)
    part_a = jax.ShapeDtypeStruct((NY, NX, piece + NZ, rank), jnp.float32)
    part_b = jax.ShapeDtypeStruct((NX, NY, piece, rank), jnp.float32)

    def spec_a(base):
        return pl.BlockSpec(
            (1,) + part_a.shape[1:], lambda i, s: (s[base + jnp.maximum(i - LOADS, 0)], 0, 0, 0)
        )

    def spec_b(base):
        return pl.BlockSpec(
            (NX, 1) + part_b.shape[2:], lambda i, s: (0, s[base + jnp.maximum(i - LOADS, 0)], 0, 0)
        )

    return pl.pallas_call(
        products_kernel,
        grid_spec=pltpu.PrefetchScalarGridSpec(
            num_scalar_prefetch=1,
            grid=(LOADS + NY,),
            in_specs=[
                pl.BlockSpec((rows, width // LOADS), lambda i, s: (0, jnp.minimum(i, LOADS - 1))),
                pl.BlockSpec((width // LOADS, rank), lambda i, s: (jnp.minimum(i, LOADS - 1), 0)),
            ],
            out_specs=(
                pl.BlockSpec((rows, rank), lambda i, s: (0, 0)),
                spec_a(1),
                spec_b(1),
                spec_a(1 + NY),
                spec_b(1 + NY),
            ),
            scratch_shapes=[
                pltpu.VMEM((NY, rows, wide), jnp.bfloat16),
                pltpu.VMEM((NY, rows, wide), jnp.bfloat16),
                pltpu.VMEM((rank, rank), jnp.float32),
                pltpu.VMEM((rows, rank), jnp.bfloat16),
                pltpu.VMEM((rows, rank), jnp.bfloat16),
            ],
        ),
        out_shape=(
            jax.ShapeDtypeStruct((rows, rank), jnp.float32), part_a, part_b, part_a, part_b
        ),
        compiler_params=pltpu.CompilerParams(vmem_limit_bytes=VMEM_LIMIT),
        cost_estimate=pl.CostEstimate(
            flops=12 * rows * width * rank, bytes_accessed=24 * 2**20, transcendentals=0
        ),
    )(slots, embeddings, matrix)


def join(core_ref, mine_ref, other_ref, out_ref):
    half = mine_ref.shape[0]
    first = core_ref[0] == 0
    out_ref[:half, :] = jnp.where(first, mine_ref[...], other_ref[...])
    out_ref[half:, :] = jnp.where(first, other_ref[...], mine_ref[...])


def eliminate(out_ref, left, right):
    order = left.shape[0]
    sub = lax.broadcasted_iota(jnp.int32, (GROUP, LANES), 0)
    halves = order // LANES
    for start in range(0, order, PANEL):
        home = start // LANES
        rows = pl.ds(start, PANEL)
        left_at = list(range(home, halves))
        right_at = list(range(0, home + 1))
        tiles = [left[rows, pl.ds(h * LANES, LANES)] for h in left_at]
        tiles += [right[rows, pl.ds(h * LANES, LANES)] for h in right_at]
        done = [[] for _ in tiles]
        pivots = []
        for group in range(0, PANEL, GROUP):
            lane = start + group - home * LANES
            tall = tiles[0].shape[0]
            cols = [
                jnp.broadcast_to(tiles[0][:, lane + m : lane + m + 1], (tall, LANES))
                for m in range(GROUP)
            ]
            for j in range(GROUP):
                pivot = cols[j][j : j + 1, :]
                pivots.append(pivot)
                low = jnp.where(sub > j, cols[j][:GROUP], 0.0)
                if tall > GROUP:
                    low = jnp.concatenate([low, cols[j][GROUP:]], axis=0)
                pivot = 1.0 / pivot
                tiles = [t - low * (t[j : j + 1, :] * pivot) for t in tiles]
                cols = [
                    q if m <= j else q - low * (q[j : j + 1, :] * pivot) for m, q in enumerate(cols)
                ]
            for i, t in enumerate(tiles):
                done[i].append(t[:GROUP])
            tiles = [t[GROUP:] for t in tiles]
        scale = lax.rsqrt(jnp.concatenate(pivots, axis=0))
        full = [jnp.concatenate(d, axis=0) * scale for d in done]
        for h, t in zip(right_at, full[len(left_at) :]):
            out_ref[rows, pl.ds(h * LANES, LANES)] = t
        below = start + PANEL
        for i, h in enumerate(left_at):
            first = max(below, h * LANES)
            if first >= (h + 1) * LANES:
                continue
            target = pl.ds(first, (h + 1) * LANES - first)
            flipped = full[i].T[first - h * LANES :]
            for k, g in enumerate(left_at):
                if g >= h:
                    left[target, pl.ds(g * LANES, LANES)] -= nn(flipped, full[k])
            for k, g in enumerate(right_at):
                right[target, pl.ds(g * LANES, LANES)] -= nn(flipped, full[len(left_at) + k])


def basis_kernel(
    scale, slots_ref, mine_ref, other_ref, sketch_ref, part_0, part_1, part_2, part_3, inverse_ref,
    basis_ref, out_ref, left, right, rows,
):
    order = left.shape[0]
    join(slots_ref, mine_ref, other_ref, left)
    for r, part in enumerate((part_0, part_1, part_2, part_3)):
        size = part.shape[0]
        at = pl.multiple_of((slots_ref[slots_ref.shape[0] - 1] ^ r) * size, size)
        rows[pl.ds(at, size), :] = part[...]
    across = lax.broadcasted_iota(jnp.int32, (order, order), 1)
    down = lax.broadcasted_iota(jnp.int32, (order, order), 0)
    right[...] = jnp.where(across == down, 1.0, 0.0)
    inverse_ref[...] = jnp.zeros_like(inverse_ref)
    eliminate(inverse_ref, left, right)
    inverse = split(inverse_ref[...])
    basis_ref[...] = three(split(sketch_ref[...]), inverse, NT) * scale
    out_ref[...] = three(split(rows[...]), inverse, NT)


def basis(slots, mine, other, sketch, parts, scale):
    order = sketch.shape[1]
    rows = jax.ShapeDtypeStruct((NX * parts[0].shape[0], order), jnp.float32)
    return pl.pallas_call(
        functools.partial(basis_kernel, scale),
        out_shape=(
            jax.ShapeDtypeStruct((order, order), jnp.float32),
            jax.ShapeDtypeStruct(sketch.shape, jnp.float32),
            rows,
        ),
        in_specs=[pl.BlockSpec(memory_space=pltpu.SMEM)]
        + [pl.BlockSpec(memory_space=pltpu.VMEM)] * (3 + NX),
        scratch_shapes=[pltpu.VMEM((order, order), jnp.float32)] * 2
        + [pltpu.VMEM(rows.shape, jnp.float32)],
        compiler_params=pltpu.CompilerParams(vmem_limit_bytes=SMALL_LIMIT),
        cost_estimate=pl.CostEstimate(flops=10**10, bytes_accessed=2**21, transcendentals=0),
    )(slots, mine, other, sketch, *parts)


def whiten_kernel(width, slots_ref, mine_ref, other_ref, inverse_ref, rows_ref, out_ref, inner):
    join(slots_ref, mine_ref, other_ref, inner)
    inverse = split(inverse_ref[...])
    order = inverse_ref.shape[0]
    across = lax.broadcasted_iota(jnp.int32, (order, order), 1)
    down = lax.broadcasted_iota(jnp.int32, (order, order), 0)
    diagonal = jnp.where(across == down, 1.5, 0.0)
    cross = three(split(three(inverse, split(inner[...]), NN)), inverse, NT)
    squares = jnp.sum(cross * cross, axis=0, keepdims=True)
    frob = jnp.sqrt(jnp.sum(squares, axis=1, keepdims=True))
    now = cross * (1.0 / frob)
    projected = rows_ref[...] * jnp.sqrt(width / frob)
    for step in range(PSTEPS):
        middle = split(diagonal - 0.5 * now)
        if step < PSTEPS - 1:
            halves = [now[:LANES], now[LANES:]]
            for _ in range(2):
                halves = [three(split(half), middle, NN) for half in halves]
            now = jnp.concatenate(halves, axis=0)
        projected = three(split(projected), middle, NN)
    out_ref[...] = projected


def whiten(slots, mine, other, inverse, block_rows, width):
    order = inverse.shape[0]
    return pl.pallas_call(
        functools.partial(whiten_kernel, width),
        out_shape=jax.ShapeDtypeStruct(block_rows.shape, jnp.float32),
        in_specs=[pl.BlockSpec(memory_space=pltpu.SMEM)]
        + [pl.BlockSpec(memory_space=pltpu.VMEM)] * 4,
        scratch_shapes=[pltpu.VMEM((order, order), jnp.float32)],
        compiler_params=pltpu.CompilerParams(vmem_limit_bytes=SMALL_LIMIT),
        cost_estimate=pl.CostEstimate(flops=10**10, bytes_accessed=2**20, transcendentals=0),
    )(slots, mine, other, inverse, block_rows)


def to_core(block):
    return lax.ppermute(block, "c", [(0, 1), (1, 0)])


def along_x(block, flip):
    return lax.ppermute(block, "x", [(x, x ^ flip) for x in range(NX)])


def exchange(blocks, axes):
    return lax.all_to_all(blocks, axes, 0, 0, tiled=True)


def ring_pairs(block, axis, turn):
    pairs = []
    for c in range(NC):
        flip = 1 if turn == c else 3
        pairs += [(c * 4 + i, c * 4 + (i ^ flip)) for i in range(4)]
    if axis == "y":
        return lax.ppermute(block, ("c", "y"), pairs)
    pairs = [((i % 4) * NC + i // 4, (j % 4) * NC + j // 4) for i, j in pairs]
    return lax.ppermute(block, ("x", "c"), pairs)


def ring_slots(core, here):
    apart = jnp.arange(4, dtype=jnp.int32) ^ here
    return jnp.where((core == 1) & (apart % 2 == 1), 4 - apart, apart)


def ring_sums(terms_a, terms_b, axis_a, axis_b):
    def first(terms, slot):
        return functools.reduce(lambda p, q: p + q, [t[slot] for t in terms])

    out = []
    sent = [sum(t[1:3] for t in terms) for terms in (terms_a, terms_b)]
    got = [ring_pairs(v, axis, 0) for v, axis in zip(sent, (axis_a, axis_b))]
    sent = [first(terms, 3) + g[1] for terms, g in zip((terms_a, terms_b), got)]
    more = [ring_pairs(v, axis, 1) for v, axis in zip(sent, (axis_a, axis_b))]
    for terms, g, m in zip((terms_a, terms_b), got, more):
        out.append([first(terms, 0), g[0], m])
    return out


def per_device(embeddings, sketch_matrix):
    rank = sketch_matrix.shape[1]
    width = embeddings.shape[1]
    share = width // (NX * NC * NY * NZ)
    total_rows = embeddings.shape[0] * NX * NC * NY * NZ
    chips = NX * NY * NZ
    x, c, y = (lax.axis_index(name).astype(jnp.int32) for name in ("x", "c", "y"))
    first_core = c == 0
    core = c.reshape(1)

    slots = jnp.concatenate(
        [core] + [ring_slots(k, at) for at in (y, x) for k in (c, 1 - c)] + [x.reshape(1)]
    )
    sketch, keep_a, keep_b, send_a, send_b = products(slots, embeddings, sketch_matrix)
    got_a, got_b = to_core(send_a), to_core(send_b)
    line_a, line_b = ring_sums([keep_a, got_a], [keep_b, got_b], "y", "x")
    own_a, own_b = ring_sums(line_a, line_b, "x", "y")
    own_a, own_b = sum(own_a), sum(own_b)
    size = own_b.shape[0]
    line = jnp.concatenate([own_a[:size], own_b]).reshape(NZ, share, rank)
    line = jnp.concatenate([line, own_a[size:][:, None]], axis=1)
    own = jnp.sum(exchange(line, "z"), axis=0)
    own_product, own_gram = own[:share], own[share:]

    from_core = to_core(own_product)
    pair = jnp.concatenate(
        [
            jnp.where(first_core, own_product, from_core),
            jnp.where(first_core, from_core, own_product),
        ]
    )
    half = jnp.where(first_core, pair[:, :chips], pair[:, chips:])
    inner = tn(half, pair)
    packet = jnp.concatenate([inner, jnp.broadcast_to(own_gram, inner.shape)], axis=1)
    packet, *parts = lax.optimization_barrier(
        (exchange(packet, CHIPS), pair, *(along_x(pair, r) for r in (1, 2, 3)))
    )
    gram = packet[:, rank:]
    inner_row = jnp.sum(packet[:, :rank], axis=0, keepdims=True)
    inner = exchange(jnp.broadcast_to(inner_row, inner.shape), CHIPS)
    inverse, left_basis, projected = basis(
        slots, gram, to_core(gram), sketch, parts, math.sqrt(total_rows)
    )
    inner, inverse = lax.optimization_barrier((inner, inverse))
    right_basis = whiten(slots, inner, to_core(inner), inverse, projected, width)
    return (left_basis, right_basis)


def solution(mesh):
    fine = Mesh(mesh.devices.reshape(NX, NC, NY, NZ), AXES)
    return jax.shard_map(
        per_device,
        mesh=fine,
        in_specs=(P(AXES, None), P()),
        out_specs=(P(AXES, None), P(("y", "z"), None)),
        check_vma=False,
    )
```

```python
import functools
import math

import jax
import jax.numpy as jnp
from jax import lax
from jax.experimental import pallas as pl
from jax.experimental.pallas import tpu as pltpu
from jax.sharding import Mesh
from jax.sharding import PartitionSpec as P

PSTEPS = 6
NX, NC, NY, NZ = 4, 2, 4, 8
LOADS = 2
AXES = ("x", "c", "y", "z")
CHIPS = ("x", "y", "z")
PANEL, GROUP, LANES = 64, 16, 128
HIGHEST = lax.Precision.HIGHEST
VMEM_LIMIT = 48 * 2**20
SMALL_LIMIT = 16 * 2**20
NN, TN, NT = ((1,), (0,)), ((0,), (0,)), ((1,), (1,))


def dot(a, b, dims, precision=None):
    return lax.dot_general(
        a, b, (dims, ((), ())), precision=precision, preferred_element_type=jnp.float32
    )


def nn(a, b):
    return dot(a, b, ((1,), (0,)), HIGHEST)


def tn(a, b):
    return dot(a, b, ((0,), (0,)), HIGHEST)


def nt(a, b):
    return dot(a, b, ((1,), (1,)), HIGHEST)


def split(value):
    high = value.astype(jnp.bfloat16)
    return high, (value - high.astype(jnp.float32)).astype(jnp.bfloat16)


def three(a, b, dims):
    return dot(a[0], b[0], dims) + (dot(a[0], b[1], dims) + dot(a[1], b[0], dims))


def products_kernel(
    slots_ref, emb_ref, matrix_ref, sketch_ref, keep_a, keep_b, send_a, send_b, high, low, gram,
    s_high, s_low,
):
    step = pl.program_id(0)
    rank = matrix_ref.shape[1]
    wide = high.shape[2]

    @pl.when(step < LOADS)
    def _():
        parts = split(emb_ref[...])
        for k in range(NY // LOADS):
            at = step * (NY // LOADS) + k
            high[at] = parts[0][:, k * wide : (k + 1) * wide]
            low[at] = parts[1][:, k * wide : (k + 1) * wide]
        term = three(parts, split(matrix_ref[...]), NN)

        @pl.when(step == 0)
        def _():
            sketch_ref[...] = term

        @pl.when(step > 0)
        def _():
            sketch_ref[...] += term

    @pl.when(step == LOADS)
    def _():
        sketch = sketch_ref[...]
        s_high[...], s_low[...] = split(sketch)
        gram[...] = tn(sketch, sketch)

    @pl.when(step >= LOADS)
    def _():
        y = step - LOADS
        product = three((high[y], low[y]), (s_high[...], s_low[...]), TN)
        product = product.reshape(NZ, NX, NC, -1, rank)
        first = slots_ref[0] == 0
        for x in range(NX):
            halves = [product[:, x, c].reshape(-1, rank) for c in range(NC)]
            extra = [
                gram[pl.ds(pl.multiple_of(NZ * ((c * NX + x) * NY + y), NZ), NZ), :]
                for c in range(NC)
            ]
            size = halves[0].shape[0] // 2
            kept = jnp.where(first, halves[0], halves[1])
            sent = jnp.where(first, halves[1], halves[0])
            keep_x, send_x = slots_ref[1 + 2 * NY + x], slots_ref[1 + 2 * NY + NX + x]
            keep_a[0, keep_x, :size, :] = kept[:size]
            send_a[0, send_x, :size, :] = sent[:size]
            keep_a[0, keep_x, size:, :] = jnp.where(first, extra[0], extra[1])
            send_a[0, send_x, size:, :] = jnp.where(first, extra[1], extra[0])
            keep_b[keep_x, 0] = kept[size:]
            send_b[send_x, 0] = sent[size:]


def products(slots, embeddings, matrix):
    rows, width = embeddings.shape
    rank = matrix.shape[1]
    wide = width // NY
    piece = wide // (NX * NC * 2)
    part_a = jax.ShapeDtypeStruct((NY, NX, piece + NZ, rank), jnp.float32)
    part_b = jax.ShapeDtypeStruct((NX, NY, piece, rank), jnp.float32)

    def spec_a(base):
        return pl.BlockSpec(
            (1,) + part_a.shape[1:], lambda i, s: (s[base + jnp.maximum(i - LOADS, 0)], 0, 0, 0)
        )

    def spec_b(base):
        return pl.BlockSpec(
            (NX, 1) + part_b.shape[2:], lambda i, s: (0, s[base + jnp.maximum(i - LOADS, 0)], 0, 0)
        )

    return pl.pallas_call(
        products_kernel,
        grid_spec=pltpu.PrefetchScalarGridSpec(
            num_scalar_prefetch=1,
            grid=(LOADS + NY,),
            in_specs=[
                pl.BlockSpec((rows, width // LOADS), lambda i, s: (0, jnp.minimum(i, LOADS - 1))),
                pl.BlockSpec((width // LOADS, rank), lambda i, s: (jnp.minimum(i, LOADS - 1), 0)),
            ],
            out_specs=(
                pl.BlockSpec((rows, rank), lambda i, s: (0, 0)),
                spec_a(1),
                spec_b(1),
                spec_a(1 + NY),
                spec_b(1 + NY),
            ),
            scratch_shapes=[
                pltpu.VMEM((NY, rows, wide), jnp.bfloat16),
                pltpu.VMEM((NY, rows, wide), jnp.bfloat16),
                pltpu.VMEM((rank, rank), jnp.float32),
                pltpu.VMEM((rows, rank), jnp.bfloat16),
                pltpu.VMEM((rows, rank), jnp.bfloat16),
            ],
        ),
        out_shape=(
            jax.ShapeDtypeStruct((rows, rank), jnp.float32), part_a, part_b, part_a, part_b
        ),
        compiler_params=pltpu.CompilerParams(vmem_limit_bytes=VMEM_LIMIT),
        cost_estimate=pl.CostEstimate(
            flops=12 * rows * width * rank, bytes_accessed=24 * 2**20, transcendentals=0
        ),
    )(slots, embeddings, matrix)


def join(core_ref, mine_ref, other_ref, out_ref):
    half = mine_ref.shape[0]
    first = core_ref[0] == 0
    out_ref[:half, :] = jnp.where(first, mine_ref[...], other_ref[...])
    out_ref[half:, :] = jnp.where(first, other_ref[...], mine_ref[...])


def eliminate(out_ref, left, right):
    order = left.shape[0]
    sub = lax.broadcasted_iota(jnp.int32, (GROUP, LANES), 0)
    halves = order // LANES
    for start in range(0, order, PANEL):
        home = start // LANES
        rows = pl.ds(start, PANEL)
        left_at = list(range(home, halves))
        right_at = list(range(0, home + 1))
        tiles = [left[rows, pl.ds(h * LANES, LANES)] for h in left_at]
        tiles += [right[rows, pl.ds(h * LANES, LANES)] for h in right_at]
        done = [[] for _ in tiles]
        pivots = []
        for group in range(0, PANEL, GROUP):
            lane = start + group - home * LANES
            tall = tiles[0].shape[0]
            cols = [
                jnp.broadcast_to(tiles[0][:, lane + m : lane + m + 1], (tall, LANES))
                for m in range(GROUP)
            ]
            for j in range(GROUP):
                pivot = cols[j][j : j + 1, :]
                pivots.append(pivot)
                low = jnp.where(sub > j, cols[j][:GROUP], 0.0)
                if tall > GROUP:
                    low = jnp.concatenate([low, cols[j][GROUP:]], axis=0)
                pivot = 1.0 / pivot
                tiles = [t - low * (t[j : j + 1, :] * pivot) for t in tiles]
                cols = [
                    q if m <= j else q - low * (q[j : j + 1, :] * pivot) for m, q in enumerate(cols)
                ]
            for i, t in enumerate(tiles):
                done[i].append(t[:GROUP])
            tiles = [t[GROUP:] for t in tiles]
        scale = lax.rsqrt(jnp.concatenate(pivots, axis=0))
        full = [jnp.concatenate(d, axis=0) * scale for d in done]
        for h, t in zip(right_at, full[len(left_at) :]):
            out_ref[rows, pl.ds(h * LANES, LANES)] = t
        below = start + PANEL
        for i, h in enumerate(left_at):
            first = max(below, h * LANES)
            if first >= (h + 1) * LANES:
                continue
            target = pl.ds(first, (h + 1) * LANES - first)
            flipped = full[i].T[first - h * LANES :]
            for k, g in enumerate(left_at):
                if g >= h:
                    left[target, pl.ds(g * LANES, LANES)] -= nn(flipped, full[k])
            for k, g in enumerate(right_at):
                right[target, pl.ds(g * LANES, LANES)] -= nn(flipped, full[len(left_at) + k])


def basis_kernel(
    scale, slots_ref, mine_ref, other_ref, sketch_ref, part_0, part_1, part_2, part_3, inverse_ref,
    basis_ref, out_ref, left, right, rows,
):
    order = left.shape[0]
    join(slots_ref, mine_ref, other_ref, left)
    for r, part in enumerate((part_0, part_1, part_2, part_3)):
        size = part.shape[0]
        at = pl.multiple_of((slots_ref[slots_ref.shape[0] - 1] ^ r) * size, size)
        rows[pl.ds(at, size), :] = part[...]
    across = lax.broadcasted_iota(jnp.int32, (order, order), 1)
    down = lax.broadcasted_iota(jnp.int32, (order, order), 0)
    right[...] = jnp.where(across == down, 1.0, 0.0)
    inverse_ref[...] = jnp.zeros_like(inverse_ref)
    eliminate(inverse_ref, left, right)
    inverse = split(inverse_ref[...])
    basis_ref[...] = three(split(sketch_ref[...]), inverse, NT) * scale
    out_ref[...] = three(split(rows[...]), inverse, NT)


def basis(slots, mine, other, sketch, parts, scale):
    order = sketch.shape[1]
    rows = jax.ShapeDtypeStruct((NX * parts[0].shape[0], order), jnp.float32)
    return pl.pallas_call(
        functools.partial(basis_kernel, scale),
        out_shape=(
            jax.ShapeDtypeStruct((order, order), jnp.float32),
            jax.ShapeDtypeStruct(sketch.shape, jnp.float32),
            rows,
        ),
        in_specs=[pl.BlockSpec(memory_space=pltpu.SMEM)]
        + [pl.BlockSpec(memory_space=pltpu.VMEM)] * (3 + NX),
        scratch_shapes=[pltpu.VMEM((order, order), jnp.float32)] * 2
        + [pltpu.VMEM(rows.shape, jnp.float32)],
        compiler_params=pltpu.CompilerParams(vmem_limit_bytes=SMALL_LIMIT),
        cost_estimate=pl.CostEstimate(flops=10**10, bytes_accessed=2**21, transcendentals=0),
    )(slots, mine, other, sketch, *parts)


def whiten_kernel(width, slots_ref, mine_ref, other_ref, inverse_ref, rows_ref, out_ref, inner):
    join(slots_ref, mine_ref, other_ref, inner)
    inverse = split(inverse_ref[...])
    order = inverse_ref.shape[0]
    across = lax.broadcasted_iota(jnp.int32, (order, order), 1)
    down = lax.broadcasted_iota(jnp.int32, (order, order), 0)
    diagonal = jnp.where(across == down, 1.5, 0.0)
    cross = three(split(three(inverse, split(inner[...]), NN)), inverse, NT)
    squares = jnp.sum(cross * cross, axis=0, keepdims=True)
    frob = jnp.sqrt(jnp.sum(squares, axis=1, keepdims=True))
    now = cross * (1.0 / frob)
    projected = rows_ref[...] * jnp.sqrt(width / frob)
    for step in range(PSTEPS):
        middle = split(diagonal - 0.5 * now)
        if step < PSTEPS - 1:
            halves = [now[:LANES], now[LANES:]]
            for _ in range(2):
                halves = [three(split(half), middle, NN) for half in halves]
            now = jnp.concatenate(halves, axis=0)
        projected = three(split(projected), middle, NN)
    out_ref[...] = projected


def whiten(slots, mine, other, inverse, block_rows, width):
    order = inverse.shape[0]
    return pl.pallas_call(
        functools.partial(whiten_kernel, width),
        out_shape=jax.ShapeDtypeStruct(block_rows.shape, jnp.float32),
        in_specs=[pl.BlockSpec(memory_space=pltpu.SMEM)]
        + [pl.BlockSpec(memory_space=pltpu.VMEM)] * 4,
        scratch_shapes=[pltpu.VMEM((order, order), jnp.float32)],
        compiler_params=pltpu.CompilerParams(vmem_limit_bytes=SMALL_LIMIT),
        cost_estimate=pl.CostEstimate(flops=10**10, bytes_accessed=2**20, transcendentals=0),
    )(slots, mine, other, inverse, block_rows)


def to_core(block):
    return lax.ppermute(block, "c", [(0, 1), (1, 0)])


def along_x(block, flip):
    return lax.ppermute(block, "x", [(x, x ^ flip) for x in range(NX)])


def exchange(blocks, axes):
    return lax.all_to_all(blocks, axes, 0, 0, tiled=True)


def ring_pairs(block, axis, turn):
    pairs = []
    for c in range(NC):
        flip = 1 if turn == c else 3
        pairs += [(c * 4 + i, c * 4 + (i ^ flip)) for i in range(4)]
    if axis == "y":
        return lax.ppermute(block, ("c", "y"), pairs)
    pairs = [((i % 4) * NC + i // 4, (j % 4) * NC + j // 4) for i, j in pairs]
    return lax.ppermute(block, ("x", "c"), pairs)


def ring_slots(core, here):
    apart = jnp.arange(4, dtype=jnp.int32) ^ here
    return jnp.where((core == 1) & (apart % 2 == 1), 4 - apart, apart)


def by_slot(blocks):
    return blocks[1:3], blocks[3], blocks[0]


def ring_sums(terms_a, terms_b, axis_a, axis_b):
    out = []
    for terms, axis in ((terms_a, axis_a), (terms_b, axis_b)):
        middle, third, own = (sum(t[k] for t in terms) for k in range(3))
        got = ring_pairs(middle, axis, 0)
        out.append([own, got[0], ring_pairs(third + got[1], axis, 1)])
    return out


def per_device(embeddings, sketch_matrix):
    rank = sketch_matrix.shape[1]
    width = embeddings.shape[1]
    share = width // (NX * NC * NY * NZ)
    total_rows = embeddings.shape[0] * NX * NC * NY * NZ
    chips = NX * NY * NZ
    x, c, y = (lax.axis_index(name).astype(jnp.int32) for name in ("x", "c", "y"))
    first_core = c == 0
    core = c.reshape(1)

    slots = jnp.concatenate(
        [core] + [ring_slots(k, at) for at in (y, x) for k in (c, 1 - c)] + [x.reshape(1)]
    )
    sketch, keep_a, keep_b, send_a, send_b = products(slots, embeddings, sketch_matrix)
    terms = []
    for keep, send in ((keep_a, send_a), (keep_b, send_b)):
        middle, third, own = by_slot(send)
        rest = to_core(jnp.stack([third, own]))
        terms.append([by_slot(keep), (to_core(middle), rest[0], rest[1])])
    line_a, line_b = ring_sums(*terms, "y", "x")
    line_a, line_b = ([by_slot(v) for v in line] for line in (line_a, line_b))
    own_a, own_b = ring_sums(line_a, line_b, "x", "y")
    own_a, own_b = sum(own_a), sum(own_b)
    size = own_b.shape[0]
    line = jnp.concatenate([own_a[:size], own_b]).reshape(NZ, share, rank)
    line = jnp.concatenate([line, own_a[size:][:, None]], axis=1)
    own = jnp.sum(exchange(line, "z"), axis=0)
    own_product, own_gram = own[:share], own[share:]

    from_core = to_core(own_product)
    pair = jnp.concatenate(
        [
            jnp.where(first_core, own_product, from_core),
            jnp.where(first_core, from_core, own_product),
        ]
    )
    half = jnp.where(first_core, pair[:, :chips], pair[:, chips:])
    inner = tn(half, pair)
    packet = jnp.concatenate([inner, jnp.broadcast_to(own_gram, inner.shape)], axis=1)
    packet, *parts = lax.optimization_barrier(
        (exchange(packet, CHIPS), pair, *(along_x(pair, r) for r in (1, 2, 3)))
    )
    gram = packet[:, rank:]
    inner_row = jnp.sum(packet[:, :rank], axis=0, keepdims=True)
    inner = exchange(jnp.broadcast_to(inner_row, inner.shape), CHIPS)
    inverse, left_basis, projected = basis(
        slots, gram, to_core(gram), sketch, parts, math.sqrt(total_rows)
    )
    inner, inverse = lax.optimization_barrier((inner, inverse))
    right_basis = whiten(slots, inner, to_core(inner), inverse, projected, width)
    return (left_basis, right_basis)


def solution(mesh):
    fine = Mesh(mesh.devices.reshape(NX, NC, NY, NZ), AXES)
    return jax.shard_map(
        per_device,
        mesh=fine,
        in_specs=(P(AXES, None), P()),
        out_specs=(P(AXES, None), P(("y", "z"), None)),
        check_vma=False,
    )
```

```python
import functools
import math

import jax
import jax.numpy as jnp
from jax import lax
from jax.experimental import pallas as pl
from jax.experimental.pallas import tpu as pltpu
from jax.sharding import Mesh
from jax.sharding import PartitionSpec as P

PSTEPS = 6
NX, NC, NY, NZ = 4, 2, 4, 8
LOADS = 2
AXES = ("x", "c", "y", "z")
CHIPS = ("x", "y", "z")
PANEL, GROUP, LANES = 64, 16, 128
HIGHEST = lax.Precision.HIGHEST
VMEM_LIMIT = 48 * 2**20
SMALL_LIMIT = 16 * 2**20
NN, TN, NT = ((1,), (0,)), ((0,), (0,)), ((1,), (1,))


def dot(a, b, dims, precision=None):
    return lax.dot_general(
        a, b, (dims, ((), ())), precision=precision, preferred_element_type=jnp.float32
    )


def nn(a, b):
    return dot(a, b, ((1,), (0,)), HIGHEST)


def tn(a, b):
    return dot(a, b, ((0,), (0,)), HIGHEST)


def nt(a, b):
    return dot(a, b, ((1,), (1,)), HIGHEST)


def split(value):
    high = value.astype(jnp.bfloat16)
    return high, (value - high.astype(jnp.float32)).astype(jnp.bfloat16)


def three(a, b, dims):
    return dot(a[0], b[0], dims) + (dot(a[0], b[1], dims) + dot(a[1], b[0], dims))


def products_kernel(
    slots_ref, emb_ref, matrix_ref, sketch_ref, keep_a, keep_b, send_a, send_b, high, low, gram,
    s_high, s_low,
):
    step = pl.program_id(0)
    rank = matrix_ref.shape[1]
    wide = high.shape[2]

    @pl.when(step < LOADS)
    def _():
        parts = split(emb_ref[...])
        for k in range(NY // LOADS):
            at = step * (NY // LOADS) + k
            high[at] = parts[0][:, k * wide : (k + 1) * wide]
            low[at] = parts[1][:, k * wide : (k + 1) * wide]
        term = three(parts, split(matrix_ref[...]), NN)

        @pl.when(step == 0)
        def _():
            sketch_ref[...] = term

        @pl.when(step > 0)
        def _():
            sketch_ref[...] += term

    @pl.when(step == LOADS)
    def _():
        sketch = sketch_ref[...]
        s_high[...], s_low[...] = split(sketch)
        gram[...] = tn(sketch, sketch)

    @pl.when(step >= LOADS)
    def _():
        y = step - LOADS
        product = three((high[y], low[y]), (s_high[...], s_low[...]), TN)
        product = product.reshape(NZ, NX, NC, -1, rank)
        first = slots_ref[0] == 0
        for x in range(NX):
            halves = [product[:, x, c].reshape(-1, rank) for c in range(NC)]
            extra = [
                gram[pl.ds(pl.multiple_of(NZ * ((c * NX + x) * NY + y), NZ), NZ), :]
                for c in range(NC)
            ]
            size = halves[0].shape[0] // 2
            kept = jnp.where(first, halves[0], halves[1])
            sent = jnp.where(first, halves[1], halves[0])
            keep_x, send_x = slots_ref[1 + 2 * NY + x], slots_ref[1 + 2 * NY + NX + x]
            keep_a[0, keep_x, :size, :] = kept[:size]
            send_a[0, send_x, :size, :] = sent[:size]
            keep_a[0, keep_x, size:, :] = jnp.where(first, extra[0], extra[1])
            send_a[0, send_x, size:, :] = jnp.where(first, extra[1], extra[0])
            keep_b[keep_x, 0] = kept[size:]
            send_b[send_x, 0] = sent[size:]


def products(slots, embeddings, matrix):
    rows, width = embeddings.shape
    rank = matrix.shape[1]
    wide = width // NY
    piece = wide // (NX * NC * 2)
    part_a = jax.ShapeDtypeStruct((NY, NX, piece + NZ, rank), jnp.float32)
    part_b = jax.ShapeDtypeStruct((NX, NY, piece, rank), jnp.float32)

    def spec_a(base):
        return pl.BlockSpec(
            (1,) + part_a.shape[1:], lambda i, s: (s[base + jnp.maximum(i - LOADS, 0)], 0, 0, 0)
        )

    def spec_b(base):
        return pl.BlockSpec(
            (NX, 1) + part_b.shape[2:], lambda i, s: (0, s[base + jnp.maximum(i - LOADS, 0)], 0, 0)
        )

    return pl.pallas_call(
        products_kernel,
        grid_spec=pltpu.PrefetchScalarGridSpec(
            num_scalar_prefetch=1,
            grid=(LOADS + NY,),
            in_specs=[
                pl.BlockSpec((rows, width // LOADS), lambda i, s: (0, jnp.minimum(i, LOADS - 1))),
                pl.BlockSpec((width // LOADS, rank), lambda i, s: (jnp.minimum(i, LOADS - 1), 0)),
            ],
            out_specs=(
                pl.BlockSpec((rows, rank), lambda i, s: (0, 0)),
                spec_a(1),
                spec_b(1),
                spec_a(1 + NY),
                spec_b(1 + NY),
            ),
            scratch_shapes=[
                pltpu.VMEM((NY, rows, wide), jnp.bfloat16),
                pltpu.VMEM((NY, rows, wide), jnp.bfloat16),
                pltpu.VMEM((rank, rank), jnp.float32),
                pltpu.VMEM((rows, rank), jnp.bfloat16),
                pltpu.VMEM((rows, rank), jnp.bfloat16),
            ],
        ),
        out_shape=(
            jax.ShapeDtypeStruct((rows, rank), jnp.float32), part_a, part_b, part_a, part_b
        ),
        compiler_params=pltpu.CompilerParams(vmem_limit_bytes=VMEM_LIMIT),
        cost_estimate=pl.CostEstimate(
            flops=12 * rows * width * rank, bytes_accessed=24 * 2**20, transcendentals=0
        ),
    )(slots, embeddings, matrix)


def join(core_ref, mine_ref, other_ref, out_ref):
    half = mine_ref.shape[0]
    first = core_ref[0] == 0
    out_ref[:half, :] = jnp.where(first, mine_ref[...], other_ref[...])
    out_ref[half:, :] = jnp.where(first, other_ref[...], mine_ref[...])


def eliminate(out_ref, left, right):
    order = left.shape[0]
    sub = lax.broadcasted_iota(jnp.int32, (GROUP, LANES), 0)
    halves = order // LANES
    for start in range(0, order, PANEL):
        home = start // LANES
        rows = pl.ds(start, PANEL)
        left_at = list(range(home, halves))
        right_at = list(range(0, home + 1))
        tiles = [left[rows, pl.ds(h * LANES, LANES)] for h in left_at]
        tiles += [right[rows, pl.ds(h * LANES, LANES)] for h in right_at]
        done = [[] for _ in tiles]
        pivots = []
        for group in range(0, PANEL, GROUP):
            lane = start + group - home * LANES
            tall = tiles[0].shape[0]
            cols = [
                jnp.broadcast_to(tiles[0][:, lane + m : lane + m + 1], (tall, LANES))
                for m in range(GROUP)
            ]
            for j in range(GROUP):
                pivot = cols[j][j : j + 1, :]
                pivots.append(pivot)
                low = jnp.where(sub > j, cols[j][:GROUP], 0.0)
                if tall > GROUP:
                    low = jnp.concatenate([low, cols[j][GROUP:]], axis=0)
                pivot = 1.0 / pivot
                tiles = [t - low * (t[j : j + 1, :] * pivot) for t in tiles]
                cols = [
                    q if m <= j else q - low * (q[j : j + 1, :] * pivot) for m, q in enumerate(cols)
                ]
            for i, t in enumerate(tiles):
                done[i].append(t[:GROUP])
            tiles = [t[GROUP:] for t in tiles]
        scale = lax.rsqrt(jnp.concatenate(pivots, axis=0))
        full = [jnp.concatenate(d, axis=0) * scale for d in done]
        for h, t in zip(right_at, full[len(left_at) :]):
            out_ref[rows, pl.ds(h * LANES, LANES)] = t
        below = start + PANEL
        for i, h in enumerate(left_at):
            first = max(below, h * LANES)
            if first >= (h + 1) * LANES:
                continue
            target = pl.ds(first, (h + 1) * LANES - first)
            flipped = full[i].T[first - h * LANES :]
            for k, g in enumerate(left_at):
                if g >= h:
                    left[target, pl.ds(g * LANES, LANES)] -= nn(flipped, full[k])
            for k, g in enumerate(right_at):
                right[target, pl.ds(g * LANES, LANES)] -= nn(flipped, full[len(left_at) + k])


def basis_kernel(
    scale, slots_ref, mine_ref, other_ref, sketch_ref, part_0, part_1, part_2, part_3, inverse_ref,
    basis_ref, out_ref, left, right, rows,
):
    order = left.shape[0]
    join(slots_ref, mine_ref, other_ref, left)
    for r, part in enumerate((part_0, part_1, part_2, part_3)):
        size = part.shape[0]
        at = pl.multiple_of((slots_ref[slots_ref.shape[0] - 1] ^ r) * size, size)
        rows[pl.ds(at, size), :] = part[...]
    across = lax.broadcasted_iota(jnp.int32, (order, order), 1)
    down = lax.broadcasted_iota(jnp.int32, (order, order), 0)
    right[...] = jnp.where(across == down, 1.0, 0.0)
    inverse_ref[...] = jnp.zeros_like(inverse_ref)
    eliminate(inverse_ref, left, right)
    inverse = split(inverse_ref[...])
    basis_ref[...] = three(split(sketch_ref[...]), inverse, NT) * scale
    out_ref[...] = three(split(rows[...]), inverse, NT)


def basis(slots, mine, other, sketch, parts, scale):
    order = sketch.shape[1]
    rows = jax.ShapeDtypeStruct((NX * parts[0].shape[0], order), jnp.float32)
    return pl.pallas_call(
        functools.partial(basis_kernel, scale),
        out_shape=(
            jax.ShapeDtypeStruct((order, order), jnp.float32),
            jax.ShapeDtypeStruct(sketch.shape, jnp.float32),
            rows,
        ),
        in_specs=[pl.BlockSpec(memory_space=pltpu.SMEM)]
        + [pl.BlockSpec(memory_space=pltpu.VMEM)] * (3 + NX),
        scratch_shapes=[pltpu.VMEM((order, order), jnp.float32)] * 2
        + [pltpu.VMEM(rows.shape, jnp.float32)],
        compiler_params=pltpu.CompilerParams(vmem_limit_bytes=SMALL_LIMIT),
        cost_estimate=pl.CostEstimate(flops=10**10, bytes_accessed=2**21, transcendentals=0),
    )(slots, mine, other, sketch, *parts)


def whiten_kernel(width, slots_ref, mine_ref, other_ref, inverse_ref, rows_ref, out_ref, inner):
    join(slots_ref, mine_ref, other_ref, inner)
    inverse = split(inverse_ref[...])
    order = inverse_ref.shape[0]
    across = lax.broadcasted_iota(jnp.int32, (order, order), 1)
    down = lax.broadcasted_iota(jnp.int32, (order, order), 0)
    diagonal = jnp.where(across == down, 1.5, 0.0)
    cross = three(split(three(inverse, split(inner[...]), NN)), inverse, NT)
    squares = jnp.sum(cross * cross, axis=0, keepdims=True)
    frob = jnp.sqrt(jnp.sum(squares, axis=1, keepdims=True))
    now = cross * (1.0 / frob)
    projected = rows_ref[...] * jnp.sqrt(width / frob)
    for step in range(PSTEPS):
        middle = split(diagonal - 0.5 * now)
        if step < PSTEPS - 1:
            halves = [now[:LANES], now[LANES:]]
            for _ in range(2):
                halves = [three(split(half), middle, NN) for half in halves]
            now = jnp.concatenate(halves, axis=0)
        projected = three(split(projected), middle, NN)
    out_ref[...] = projected


def whiten(slots, mine, other, inverse, block_rows, width):
    order = inverse.shape[0]
    return pl.pallas_call(
        functools.partial(whiten_kernel, width),
        out_shape=jax.ShapeDtypeStruct(block_rows.shape, jnp.float32),
        in_specs=[pl.BlockSpec(memory_space=pltpu.SMEM)]
        + [pl.BlockSpec(memory_space=pltpu.VMEM)] * 4,
        scratch_shapes=[pltpu.VMEM((order, order), jnp.float32)],
        compiler_params=pltpu.CompilerParams(vmem_limit_bytes=SMALL_LIMIT),
        cost_estimate=pl.CostEstimate(flops=10**10, bytes_accessed=2**20, transcendentals=0),
    )(slots, mine, other, inverse, block_rows)


def to_core(block):
    return lax.ppermute(block, "c", [(0, 1), (1, 0)])


def along_x(block, flip):
    return lax.ppermute(block, "x", [(x, x ^ flip) for x in range(NX)])


def exchange(blocks, axes):
    return lax.all_to_all(blocks, axes, 0, 0, tiled=True)


def ring_pairs(block, axis, turn):
    pairs = []
    for c in range(NC):
        flip = 1 if turn == c else 3
        pairs += [(c * 4 + i, c * 4 + (i ^ flip)) for i in range(4)]
    if axis == "y":
        return lax.ppermute(block, ("c", "y"), pairs)
    pairs = [((i % 4) * NC + i // 4, (j % 4) * NC + j // 4) for i, j in pairs]
    return lax.ppermute(block, ("x", "c"), pairs)


def ring_slots(core, here):
    apart = jnp.arange(4, dtype=jnp.int32) ^ here
    return jnp.where((core == 1) & (apart % 2 == 1), 4 - apart, apart)


def by_slot(blocks):
    return blocks[1:3], blocks[3], blocks[0]


def ring_sums(terms_a, terms_b, axis_a, axis_b, apart=False):
    out = []
    for terms, axis in ((terms_a, axis_a), (terms_b, axis_b)):
        middle, third, own = (sum(t[k] for t in terms) for k in range(3))
        if apart:
            far = ring_pairs(middle[1], axis, 0)
            far, near = lax.optimization_barrier((far, middle[0]))
            near = ring_pairs(near, axis, 0)
        else:
            near, far = ring_pairs(middle, axis, 0)
        out.append([own, near, ring_pairs(third + far, axis, 1)])
    return out


def per_device(embeddings, sketch_matrix):
    rank = sketch_matrix.shape[1]
    width = embeddings.shape[1]
    share = width // (NX * NC * NY * NZ)
    total_rows = embeddings.shape[0] * NX * NC * NY * NZ
    chips = NX * NY * NZ
    x, c, y = (lax.axis_index(name).astype(jnp.int32) for name in ("x", "c", "y"))
    first_core = c == 0
    core = c.reshape(1)

    slots = jnp.concatenate(
        [core] + [ring_slots(k, at) for at in (y, x) for k in (c, 1 - c)] + [x.reshape(1)]
    )
    sketch, keep_a, keep_b, send_a, send_b = products(slots, embeddings, sketch_matrix)
    terms = []
    for keep, send in ((keep_a, send_a), (keep_b, send_b)):
        middle, third, own = by_slot(send)
        rest = to_core(jnp.stack([third, own]))
        terms.append([by_slot(keep), (to_core(middle), rest[0], rest[1])])
    line_a, line_b = ring_sums(*terms, "y", "x", apart=True)
    line_a, line_b = ([by_slot(v) for v in line] for line in (line_a, line_b))
    own_a, own_b = ring_sums(line_a, line_b, "x", "y")
    own_a, own_b = sum(own_a), sum(own_b)
    size = own_b.shape[0]
    line = jnp.concatenate([own_a[:size], own_b]).reshape(NZ, share, rank)
    line = jnp.concatenate([line, own_a[size:][:, None]], axis=1)
    own = jnp.sum(exchange(line, "z"), axis=0)
    own_product, own_gram = own[:share], own[share:]

    from_core = to_core(own_product)
    pair = jnp.concatenate(
        [
            jnp.where(first_core, own_product, from_core),
            jnp.where(first_core, from_core, own_product),
        ]
    )
    half = jnp.where(first_core, pair[:, :chips], pair[:, chips:])
    inner = tn(half, pair)
    packet = jnp.concatenate([inner, jnp.broadcast_to(own_gram, inner.shape)], axis=1)
    packet, *parts = lax.optimization_barrier(
        (exchange(packet, CHIPS), pair, *(along_x(pair, r) for r in (1, 2, 3)))
    )
    gram = packet[:, rank:]
    inner_row = jnp.sum(packet[:, :rank], axis=0, keepdims=True)
    inner = exchange(jnp.broadcast_to(inner_row, inner.shape), CHIPS)
    inverse, left_basis, projected = basis(
        slots, gram, to_core(gram), sketch, parts, math.sqrt(total_rows)
    )
    inner, inverse = lax.optimization_barrier((inner, inverse))
    right_basis = whiten(slots, inner, to_core(inner), inverse, projected, width)
    return (left_basis, right_basis)


def solution(mesh):
    fine = Mesh(mesh.devices.reshape(NX, NC, NY, NZ), AXES)
    return jax.shard_map(
        per_device,
        mesh=fine,
        in_specs=(P(AXES, None), P()),
        out_specs=(P(AXES, None), P(("y", "z"), None)),
        check_vma=False,
    )
```

```python
import functools
import math

import jax
import jax.numpy as jnp
from jax import lax
from jax.experimental import pallas as pl
from jax.experimental.pallas import tpu as pltpu
from jax.sharding import Mesh
from jax.sharding import PartitionSpec as P

PSTEPS = 6
NX, NC, NY, NZ = 4, 2, 4, 8
LOADS = 2
AXES = ("x", "c", "y", "z")
CHIPS = ("x", "y", "z")
PANEL, GROUP, LANES = 64, 16, 128
HIGHEST = lax.Precision.HIGHEST
VMEM_LIMIT = 48 * 2**20
SMALL_LIMIT = 16 * 2**20
NN, TN, NT = ((1,), (0,)), ((0,), (0,)), ((1,), (1,))


def dot(a, b, dims, precision=None):
    return lax.dot_general(
        a, b, (dims, ((), ())), precision=precision, preferred_element_type=jnp.float32
    )


def nn(a, b):
    return dot(a, b, ((1,), (0,)), HIGHEST)


def tn(a, b):
    return dot(a, b, ((0,), (0,)), HIGHEST)


def nt(a, b):
    return dot(a, b, ((1,), (1,)), HIGHEST)


def split(value):
    high = value.astype(jnp.bfloat16)
    return high, (value - high.astype(jnp.float32)).astype(jnp.bfloat16)


def three(a, b, dims):
    return dot(a[0], b[0], dims) + (dot(a[0], b[1], dims) + dot(a[1], b[0], dims))


def products_kernel(
    slots_ref, emb_ref, matrix_ref, sketch_ref, keep_a, keep_b, send_a, send_b, high, low, gram,
    s_high, s_low,
):
    step = pl.program_id(0)
    rank = matrix_ref.shape[1]
    wide = high.shape[2]

    @pl.when(step < LOADS)
    def _():
        parts = split(emb_ref[...])
        for k in range(NY // LOADS):
            at = step * (NY // LOADS) + k
            high[at] = parts[0][:, k * wide : (k + 1) * wide]
            low[at] = parts[1][:, k * wide : (k + 1) * wide]
        term = three(parts, split(matrix_ref[...]), NN)

        @pl.when(step == 0)
        def _():
            sketch_ref[...] = term

        @pl.when(step > 0)
        def _():
            sketch_ref[...] += term

    @pl.when(step == LOADS)
    def _():
        sketch = sketch_ref[...]
        s_high[...], s_low[...] = split(sketch)
        gram[...] = tn(sketch, sketch)

    @pl.when(step >= LOADS)
    def _():
        y = step - LOADS
        product = three((high[y], low[y]), (s_high[...], s_low[...]), TN)
        product = product.reshape(NZ, NX, NC, -1, rank)
        first = slots_ref[0] == 0
        for x in range(NX):
            halves = [product[:, x, c].reshape(-1, rank) for c in range(NC)]
            extra = [
                gram[pl.ds(pl.multiple_of(NZ * ((c * NX + x) * NY + y), NZ), NZ), :]
                for c in range(NC)
            ]
            size = halves[0].shape[0] // 2
            kept = jnp.where(first, halves[0], halves[1])
            sent = jnp.where(first, halves[1], halves[0])
            keep_x, send_x = slots_ref[1 + 2 * NY + x], slots_ref[1 + 2 * NY + NX + x]
            keep_a[0, keep_x, :size, :] = kept[:size]
            send_a[0, send_x, :size, :] = sent[:size]
            keep_a[0, keep_x, size:, :] = jnp.where(first, extra[0], extra[1])
            send_a[0, send_x, size:, :] = jnp.where(first, extra[1], extra[0])
            keep_b[keep_x, 0] = kept[size:]
            send_b[send_x, 0] = sent[size:]


def products(slots, embeddings, matrix):
    rows, width = embeddings.shape
    rank = matrix.shape[1]
    wide = width // NY
    piece = wide // (NX * NC * 2)
    part_a = jax.ShapeDtypeStruct((NY, NX, piece + NZ, rank), jnp.float32)
    part_b = jax.ShapeDtypeStruct((NX, NY, piece, rank), jnp.float32)

    def spec_a(base):
        return pl.BlockSpec(
            (1,) + part_a.shape[1:], lambda i, s: (s[base + jnp.maximum(i - LOADS, 0)], 0, 0, 0)
        )

    def spec_b(base):
        return pl.BlockSpec(
            (NX, 1) + part_b.shape[2:], lambda i, s: (0, s[base + jnp.maximum(i - LOADS, 0)], 0, 0)
        )

    return pl.pallas_call(
        products_kernel,
        grid_spec=pltpu.PrefetchScalarGridSpec(
            num_scalar_prefetch=1,
            grid=(LOADS + NY,),
            in_specs=[
                pl.BlockSpec((rows, width // LOADS), lambda i, s: (0, jnp.minimum(i, LOADS - 1))),
                pl.BlockSpec((width // LOADS, rank), lambda i, s: (jnp.minimum(i, LOADS - 1), 0)),
            ],
            out_specs=(
                pl.BlockSpec((rows, rank), lambda i, s: (0, 0)),
                spec_a(1),
                spec_b(1),
                spec_a(1 + NY),
                spec_b(1 + NY),
            ),
            scratch_shapes=[
                pltpu.VMEM((NY, rows, wide), jnp.bfloat16),
                pltpu.VMEM((NY, rows, wide), jnp.bfloat16),
                pltpu.VMEM((rank, rank), jnp.float32),
                pltpu.VMEM((rows, rank), jnp.bfloat16),
                pltpu.VMEM((rows, rank), jnp.bfloat16),
            ],
        ),
        out_shape=(
            jax.ShapeDtypeStruct((rows, rank), jnp.float32), part_a, part_b, part_a, part_b
        ),
        compiler_params=pltpu.CompilerParams(vmem_limit_bytes=VMEM_LIMIT),
        cost_estimate=pl.CostEstimate(
            flops=12 * rows * width * rank, bytes_accessed=24 * 2**20, transcendentals=0
        ),
    )(slots, embeddings, matrix)


def join(core_ref, mine_ref, other_ref, out_ref):
    half = mine_ref.shape[0]
    first = core_ref[0] == 0
    out_ref[:half, :] = jnp.where(first, mine_ref[...], other_ref[...])
    out_ref[half:, :] = jnp.where(first, other_ref[...], mine_ref[...])


def eliminate(out_ref, left, right):
    order = left.shape[0]
    sub = lax.broadcasted_iota(jnp.int32, (GROUP, LANES), 0)
    halves = order // LANES
    for start in range(0, order, PANEL):
        home = start // LANES
        rows = pl.ds(start, PANEL)
        left_at = list(range(home, halves))
        right_at = list(range(0, home + 1))
        tiles = [left[rows, pl.ds(h * LANES, LANES)] for h in left_at]
        tiles += [right[rows, pl.ds(h * LANES, LANES)] for h in right_at]
        done = [[] for _ in tiles]
        pivots = []
        for group in range(0, PANEL, GROUP):
            lane = start + group - home * LANES
            tall = tiles[0].shape[0]
            cols = [
                jnp.broadcast_to(tiles[0][:, lane + m : lane + m + 1], (tall, LANES))
                for m in range(GROUP)
            ]
            for j in range(GROUP):
                pivot = cols[j][j : j + 1, :]
                pivots.append(pivot)
                low = jnp.where(sub > j, cols[j][:GROUP], 0.0)
                if tall > GROUP:
                    low = jnp.concatenate([low, cols[j][GROUP:]], axis=0)
                pivot = 1.0 / pivot
                tiles = [t - low * (t[j : j + 1, :] * pivot) for t in tiles]
                cols = [
                    q if m <= j else q - low * (q[j : j + 1, :] * pivot) for m, q in enumerate(cols)
                ]
            for i, t in enumerate(tiles):
                done[i].append(t[:GROUP])
            tiles = [t[GROUP:] for t in tiles]
        scale = lax.rsqrt(jnp.concatenate(pivots, axis=0))
        full = [jnp.concatenate(d, axis=0) * scale for d in done]
        for h, t in zip(right_at, full[len(left_at) :]):
            out_ref[rows, pl.ds(h * LANES, LANES)] = t
        below = start + PANEL
        for i, h in enumerate(left_at):
            first = max(below, h * LANES)
            if first >= (h + 1) * LANES:
                continue
            target = pl.ds(first, (h + 1) * LANES - first)
            flipped = full[i].T[first - h * LANES :]
            for k, g in enumerate(left_at):
                if g >= h:
                    left[target, pl.ds(g * LANES, LANES)] -= nn(flipped, full[k])
            for k, g in enumerate(right_at):
                right[target, pl.ds(g * LANES, LANES)] -= nn(flipped, full[len(left_at) + k])


def basis_kernel(
    scale, slots_ref, mine_ref, other_ref, sketch_ref, part_0, part_1, part_2, part_3, inverse_ref,
    basis_ref, out_ref, left, right, rows,
):
    order = left.shape[0]
    join(slots_ref, mine_ref, other_ref, left)
    for r, part in enumerate((part_0, part_1, part_2, part_3)):
        size = part.shape[0]
        at = pl.multiple_of((slots_ref[slots_ref.shape[0] - 1] ^ r) * size, size)
        rows[pl.ds(at, size), :] = part[...]
    across = lax.broadcasted_iota(jnp.int32, (order, order), 1)
    down = lax.broadcasted_iota(jnp.int32, (order, order), 0)
    right[...] = jnp.where(across == down, 1.0, 0.0)
    inverse_ref[...] = jnp.zeros_like(inverse_ref)
    eliminate(inverse_ref, left, right)
    inverse = split(inverse_ref[...])
    basis_ref[...] = three(split(sketch_ref[...]), inverse, NT) * scale
    out_ref[...] = three(split(rows[...]), inverse, NT)


def basis(slots, mine, other, sketch, parts, scale):
    order = sketch.shape[1]
    rows = jax.ShapeDtypeStruct((NX * parts[0].shape[0], order), jnp.float32)
    return pl.pallas_call(
        functools.partial(basis_kernel, scale),
        out_shape=(
            jax.ShapeDtypeStruct((order, order), jnp.float32),
            jax.ShapeDtypeStruct(sketch.shape, jnp.float32),
            rows,
        ),
        in_specs=[pl.BlockSpec(memory_space=pltpu.SMEM)]
        + [pl.BlockSpec(memory_space=pltpu.VMEM)] * (3 + NX),
        scratch_shapes=[pltpu.VMEM((order, order), jnp.float32)] * 2
        + [pltpu.VMEM(rows.shape, jnp.float32)],
        compiler_params=pltpu.CompilerParams(vmem_limit_bytes=SMALL_LIMIT),
        cost_estimate=pl.CostEstimate(flops=10**10, bytes_accessed=2**21, transcendentals=0),
    )(slots, mine, other, sketch, *parts)


def whiten_kernel(width, slots_ref, mine_ref, other_ref, inverse_ref, rows_ref, out_ref, inner):
    join(slots_ref, mine_ref, other_ref, inner)
    inverse = split(inverse_ref[...])
    order = inverse_ref.shape[0]
    across = lax.broadcasted_iota(jnp.int32, (order, order), 1)
    down = lax.broadcasted_iota(jnp.int32, (order, order), 0)
    diagonal = jnp.where(across == down, 1.5, 0.0)
    cross = three(split(three(inverse, split(inner[...]), NN)), inverse, NT)
    squares = jnp.sum(cross * cross, axis=0, keepdims=True)
    frob = jnp.sqrt(jnp.sum(squares, axis=1, keepdims=True))
    now = cross * (1.0 / frob)
    projected = rows_ref[...] * jnp.sqrt(width / frob)
    for step in range(PSTEPS):
        middle = split(diagonal - 0.5 * now)
        if step < PSTEPS - 1:
            halves = [now[:LANES], now[LANES:]]
            for _ in range(2):
                halves = [three(split(half), middle, NN) for half in halves]
            now = jnp.concatenate(halves, axis=0)
        projected = three(split(projected), middle, NN)
    out_ref[...] = projected


def whiten(slots, mine, other, inverse, block_rows, width):
    order = inverse.shape[0]
    return pl.pallas_call(
        functools.partial(whiten_kernel, width),
        out_shape=jax.ShapeDtypeStruct(block_rows.shape, jnp.float32),
        in_specs=[pl.BlockSpec(memory_space=pltpu.SMEM)]
        + [pl.BlockSpec(memory_space=pltpu.VMEM)] * 4,
        scratch_shapes=[pltpu.VMEM((order, order), jnp.float32)],
        compiler_params=pltpu.CompilerParams(vmem_limit_bytes=SMALL_LIMIT),
        cost_estimate=pl.CostEstimate(flops=10**10, bytes_accessed=2**20, transcendentals=0),
    )(slots, mine, other, inverse, block_rows)


def to_core(block):
    return lax.ppermute(block, "c", [(0, 1), (1, 0)])


def along_x(block, flip):
    return lax.ppermute(block, "x", [(x, x ^ flip) for x in range(NX)])


def exchange(blocks, axes):
    return lax.all_to_all(blocks, axes, 0, 0, tiled=True)


def ring_pairs(block, axis, turn):
    pairs = []
    for c in range(NC):
        flip = 1 if turn == c else 3
        pairs += [(c * 4 + i, c * 4 + (i ^ flip)) for i in range(4)]
    if axis == "y":
        return lax.ppermute(block, ("c", "y"), pairs)
    pairs = [((i % 4) * NC + i // 4, (j % 4) * NC + j // 4) for i, j in pairs]
    return lax.ppermute(block, ("x", "c"), pairs)


def ring_slots(core, here):
    apart = jnp.arange(4, dtype=jnp.int32) ^ here
    return jnp.where((core == 1) & (apart % 2 == 1), 4 - apart, apart)


def by_slot(blocks):
    return blocks[1:3], blocks[3], blocks[0]


def ring_sums(terms_a, terms_b, axis_a, axis_b, apart=False):
    out = []
    for terms, axis in ((terms_a, axis_a), (terms_b, axis_b)):
        middle, third, own = (sum(t[k] for t in terms) for k in range(3))
        if apart:
            far = ring_pairs(middle[1], axis, 0)
            far, near = lax.optimization_barrier((far, middle[0]))
            near = ring_pairs(near, axis, 0)
        else:
            near, far = ring_pairs(middle, axis, 0)
        out.append([own, near, ring_pairs(third + far, axis, 1)])
    return out


def per_device(embeddings, sketch_matrix):
    rank = sketch_matrix.shape[1]
    width = embeddings.shape[1]
    share = width // (NX * NC * NY * NZ)
    total_rows = embeddings.shape[0] * NX * NC * NY * NZ
    chips = NX * NY * NZ
    x, c, y = (lax.axis_index(name).astype(jnp.int32) for name in ("x", "c", "y"))
    first_core = c == 0
    core = c.reshape(1)

    slots = jnp.concatenate(
        [core] + [ring_slots(k, at) for at in (y, x) for k in (c, 1 - c)] + [x.reshape(1)]
    )
    sketch, keep_a, keep_b, send_a, send_b = products(slots, embeddings, sketch_matrix)
    terms = []
    for keep, send in ((keep_a, send_a), (keep_b, send_b)):
        middle, third, own = by_slot(send)
        rest = to_core(jnp.stack([third, own]))
        terms.append([by_slot(keep), (to_core(middle), rest[0], rest[1])])
    line_a, line_b = ring_sums(*terms, "y", "x", apart=True)
    line_a, line_b = ([by_slot(v) for v in line] for line in (line_a, line_b))
    own_a, own_b = ring_sums(line_a, line_b, "x", "y", apart=True)
    own_a, own_b = sum(own_a), sum(own_b)
    size = own_b.shape[0]
    line = jnp.concatenate([own_a[:size], own_b]).reshape(NZ, share, rank)
    line = jnp.concatenate([line, own_a[size:][:, None]], axis=1)
    own = jnp.sum(exchange(line, "z"), axis=0)
    own_product, own_gram = own[:share], own[share:]

    from_core = to_core(own_product)
    pair = jnp.concatenate(
        [
            jnp.where(first_core, own_product, from_core),
            jnp.where(first_core, from_core, own_product),
        ]
    )
    half = jnp.where(first_core, pair[:, :chips], pair[:, chips:])
    inner = tn(half, pair)
    packet = jnp.concatenate([inner, jnp.broadcast_to(own_gram, inner.shape)], axis=1)
    packet, *parts = lax.optimization_barrier(
        (exchange(packet, CHIPS), pair, *(along_x(pair, r) for r in (1, 2, 3)))
    )
    gram = packet[:, rank:]
    inner_row = jnp.sum(packet[:, :rank], axis=0, keepdims=True)
    inner = exchange(jnp.broadcast_to(inner_row, inner.shape), CHIPS)
    inverse, left_basis, projected = basis(
        slots, gram, to_core(gram), sketch, parts, math.sqrt(total_rows)
    )
    inner, inverse = lax.optimization_barrier((inner, inverse))
    right_basis = whiten(slots, inner, to_core(inner), inverse, projected, width)
    return (left_basis, right_basis)


def solution(mesh):
    fine = Mesh(mesh.devices.reshape(NX, NC, NY, NZ), AXES)
    return jax.shard_map(
        per_device,
        mesh=fine,
        in_specs=(P(AXES, None), P()),
        out_specs=(P(AXES, None), P(("y", "z"), None)),
        check_vma=False,
    )
```
